512 devices in a mesh: rep: 32 (over y, z_hi), trow: 4 (over z_lo, core), tcol: 4 (over x).
Axes of the slice: x: 4, y: 8, z: 8 (z_hi: 4, z_lo: 2; z = z_hi * 2 + z_lo), core: 2. Of those that a mesh axis runs over, the one named last changes fastest.
Arguments:
- pseudo_grads: bfloat16 [32, 5120, 1024], P('rep', 'trow', 'tcol'), may hold values from -1200 to 1200
- left_gram: float32 [16, 320, 320], P(('trow', 'tcol')), may hold values from -102.4 to 61.44
- right_gram: float32 [4, 256, 256], P('tcol'), may hold values from -512 to 307.2
- left_basis: float32 [16, 320, 320], P(('trow', 'tcol')), may hold values from -1 to 2
- right_basis: float32 [4, 256, 256], P('tcol'), may hold values from -1 to 2
- first_moment: float32 [5120, 1024], P(('trow', 'rep'), 'tcol'), may hold values from -1.8 to 1.8
- second_moment: float32 [5120, 1024], P(('trow', 'rep'), 'tcol'), may hold values from 0.05 to 1
Outputs:
- update: bfloat16 [5120, 1024], P('trow', 'tcol')
- new_left_gram: float32 [16, 320, 320], P(('trow', 'tcol'))
- new_left_basis: float32 [16, 320, 320], P(('trow', 'tcol'))
- new_right_gram: float32 [4, 256, 256], P('tcol')
- new_right_basis: float32 [4, 256, 256], P('tcol')
- new_first_moment: float32 [5120, 1024], P(('trow', 'rep'), 'tcol')
- new_second_moment: float32 [5120, 1024], P(('trow', 'rep'), 'tcol')
The draws below stay inside these ranges and needn't reach their ends.
All inputs are finite; a program needn't handle non-finite values.
Results may differ from the reference program's by a relative error of at most 0.001.
Values sent between devices are 32-bit elements; how exact they have to be, the bound alone decides.
No kernel may reach another device: no remote copies, remote signals or barrier semaphores. Data moves between devices by JAX's collectives and lax.ppermute only.
A program may use at most 64 MiB of HBM per device.

```python
import math
import jax
import jax.numpy as jnp
from jax import lax

D = 5120
KV = 1024
LB = 320
RB = 256
REPS = 32


def symmetric_blocks(key, count, width, diag_lo, diag_hi, spread):
    key_diag, key_off = jax.random.split(key)
    raw = jax.random.truncated_normal(key_off, -4.0, 4.0, (count, width, width), jnp.float32)
    sym = (raw + jnp.swapaxes(raw, 1, 2)) * (spread / math.sqrt(2.0))
    eye_mask = jnp.eye(width, dtype=jnp.float32)
    diag_vals = jax.random.uniform(key_diag, (count, width, 1), jnp.float32, diag_lo, diag_hi)
    return sym * (1.0 - eye_mask) + eye_mask * diag_vals


def near_identity(key, count, width):
    noise = jax.random.truncated_normal(key, -4.0, 4.0, (count, width, width), jnp.float32)
    return jnp.eye(width, dtype=jnp.float32)[None] + noise * (0.25 / math.sqrt(width))


def draw_pseudo_grads(key, part):
    key = jax.random.fold_in(key, 7)
    key_row, key_col, key_noise = jax.random.split(key, 3)
    row_trend = jnp.sqrt(1.0 + 2.0 * jnp.arange(D, dtype=jnp.float32) / (D - 1))
    col_trend = jnp.sqrt(1.0 + 2.0 * jnp.arange(KV, dtype=jnp.float32) / (KV - 1))
    row_scale = jnp.exp(jax.random.uniform(key_row, (D,), jnp.float32, 0.0, math.log(3.0)))
    col_scale = jnp.exp(jax.random.uniform(key_col, (KV,), jnp.float32, 0.0, math.log(3.0)))
    base = jax.random.truncated_normal(key_noise, -4.0, 4.0, (REPS, D, KV), jnp.float32)
    scaled = base * (row_scale * row_trend)[None, :, None] * (col_scale * col_trend)[None, None, :]
    return scaled.astype(jnp.bfloat16)


def draw_left_gram(key, part):
    key = jax.random.fold_in(key, 11)
    return symmetric_blocks(key, D // LB, LB, 0.04 * KV, 0.055 * KV, 0.0125 * KV / math.sqrt(LB))


def draw_right_gram(key, part):
    key = jax.random.fold_in(key, 13)
    return symmetric_blocks(key, KV // RB, RB, 0.04 * D, 0.055 * D, 0.0125 * D / math.sqrt(RB))


def draw_left_basis(key, part):
    key = jax.random.fold_in(key, 17)
    return near_identity(key, D // LB, LB)


def draw_right_basis(key, part):
    key = jax.random.fold_in(key, 19)
    return near_identity(key, KV // RB, RB)


def steps_of(stream_key, extent, cuts, low, high):
    def one(dim, shards_of):
        heights = jax.random.uniform(jax.random.fold_in(jax.random.fold_in(stream_key, 6), dim), (shards_of,), jnp.float32, low / len(cuts), high / len(cuts))
        return jnp.repeat(jnp.exp(heights), extent[dim] // shards_of).reshape((-1,) + (1,) * (len(extent) - dim - 1))

    gain = one(*cuts[0])
    for cut in cuts[1:]:
        gain = gain * one(*cut)
    return gain


def normal_values(own_key, extent, scale, limit, pieces=(), kind=jnp.bfloat16):
    values = jax.random.normal(own_key, extent, jnp.float32) * scale
    if len(pieces) > 0:
        values = steps_of(own_key, extent, pieces, -0.22, 0.18) * values
    return jnp.clip(values, min=-limit, max=limit).astype(kind)


def setup_inputs(seed: int = 0) -> dict:
    splits = jax.random.split(jax.random.key(seed), 8)
    pseudo_grads = draw_pseudo_grads(jax.random.fold_in(splits[7], 71), 0)
    left_gram = draw_left_gram(jax.random.fold_in(splits[7], 71), 0)
    right_gram = draw_right_gram(jax.random.fold_in(splits[7], 71), 0)
    left_basis = draw_left_basis(jax.random.fold_in(splits[7], 71), 0)
    right_basis = draw_right_basis(jax.random.fold_in(splits[7], 71), 0)
    first_moment = normal_values(splits[5], (D, KV), 0.3, 1.8, ((0, 128), (1, 4)), jnp.float32)
    second_moment = jnp.clip(jnp.exp(math.log(1.0) - 2.9957323 * jax.random.uniform(splits[6], (D, KV), jnp.float32) ** steps_of(splits[6], (D, KV), ((0, 128), (1, 4)), -0.2, 0.2)), 0.05, 1.0)
    return dict(pseudo_grads=pseudo_grads, left_gram=left_gram, right_gram=right_gram, left_basis=left_basis, right_basis=right_basis, first_moment=first_moment, second_moment=second_moment)


highest = lax.Precision.HIGHEST
beta_gram = 0.95
beta_first = 0.95
beta_second = 0.95
first_bias = 1.0 - 0.95 ** 4
second_bias = 1.0 - 0.95 ** 4
clip_ratio = 0.5

def refresh(gram, basis):
    powered = jnp.einsum('bij,bjk->bik', gram, basis, precision=highest)
    crossed = jnp.einsum('bki,bkj->bij', powered, powered, precision=highest)
    factor = jnp.linalg.cholesky(crossed)

    def solve_one(chol_factor, powered_block):
        return jax.scipy.linalg.solve_triangular(chol_factor, powered_block.T, lower=True).T
    return jax.vmap(solve_one)(factor, powered)

def rotate(tile_grad, left_blocks, right_blocks):
    stacked = tile_grad.reshape(left_blocks.shape[0], left_blocks.shape[1], tile_grad.shape[1])
    turned = jnp.einsum('bki,bkc->bic', left_blocks, stacked, precision=highest).reshape(tile_grad.shape)
    split_cols = turned.reshape(tile_grad.shape[0], right_blocks.shape[0], right_blocks.shape[1])
    return jnp.einsum('dbk,bkj->dbj', split_cols, right_blocks, precision=highest).reshape(tile_grad.shape)

def unrotate(tile_dir, left_blocks, right_blocks):
    stacked = tile_dir.reshape(left_blocks.shape[0], left_blocks.shape[1], tile_dir.shape[1])
    turned = jnp.einsum('bik,bkc->bic', left_blocks, stacked, precision=highest).reshape(tile_dir.shape)
    split_cols = turned.reshape(tile_dir.shape[0], right_blocks.shape[0], right_blocks.shape[1])
    return jnp.einsum('dbk,bjk->dbj', split_cols, right_blocks, precision=highest).reshape(tile_dir.shape)

def adam_step(rotated, first_moment, second_moment):
    moment = beta_first * first_moment + (1.0 - beta_first) * rotated
    second = beta_second * second_moment + (1.0 - beta_second) * rotated * rotated
    direction = moment / first_bias / (jnp.sqrt(second / second_bias) + 1e-08)
    return (moment, second, direction)

def reference(pseudo_grads, left_gram, right_gram, left_basis, right_basis, first_moment, second_moment):
    replicas = pseudo_grads.shape[0]
    average = lax.optimization_barrier(jnp.sum(pseudo_grads, axis=0, dtype=jnp.float32)) / replicas
    norm_value = jnp.sqrt(jnp.sum(average * average))
    factor = clip_ratio * math.sqrt(D * KV) / (norm_value + 1e-06)
    gradient = average * factor
    stacked = gradient.reshape(D // LB, LB, KV)
    left_new = beta_gram * left_gram + (1.0 - beta_gram) * jnp.einsum('bic,bjc->bij', stacked, stacked, precision=highest)
    columns = gradient.reshape(D, KV // RB, RB)
    right_new = beta_gram * right_gram + (1.0 - beta_gram) * jnp.einsum('dbi,dbj->bij', columns, columns, precision=highest)
    left_basis_new = refresh(left_new, left_basis)
    right_basis_new = refresh(right_new, right_basis)
    rotated = rotate(gradient, left_basis_new, right_basis_new)
    moment, second, direction = adam_step(rotated, first_moment, second_moment)
    update = unrotate(direction, left_basis_new, right_basis_new).astype(jnp.bfloat16)
    return (update, left_new, left_basis_new, right_new, right_basis_new, moment, second)
```

```python
import math

import jax
import jax.numpy as jnp
from jax import lax
from jax.experimental import pallas as pl
from jax.experimental.pallas import tpu as pltpu
from jax.sharding import Mesh, PartitionSpec as P

D = 5120
KV = 1024
LB = 320
RB = 256
NB = 64

highest = lax.Precision.HIGHEST
beta_gram = 0.95
beta_first = 0.95
beta_second = 0.95
first_bias = 1.0 - 0.95**4
second_bias = 1.0 - 0.95**4
clip_ratio = 0.5

REP = ("yk", "y2", "zh")
ROW = ("zl", "core")
MEMBERS = ("y2", "zh")
RIGHT_GROUP = ("yk", "zl", "core")


def mm(a, b, ca=1, cb=0):
    return lax.dot_general(
        a, b, (((ca,), (cb,)), ((), ())), precision=highest, preferred_element_type=jnp.float32
    )


def eliminate(rows, off):
    row_id = lax.broadcasted_iota(jnp.int32, (8, 128), 0)
    for g in range(8):
        count = 8 - g
        cols = [
            [
                jnp.broadcast_to(rows[g + h][:, off + 8 * g + t : off + 8 * g + t + 1], (8, 128))
                for h in range(count)
            ]
            for t in range(8)
        ]
        pivots = jnp.ones((8, 128), jnp.float32)
        for t in range(8):
            pivot = jnp.broadcast_to(cols[t][0][t : t + 1, :], (8, 128))
            inv = 1.0 / pivot
            pivots = jnp.where(row_id == t, pivot, pivots)
            f = [c * inv for c in cols[t]]
            f[0] = jnp.where(row_id > t, f[0], 0.0)
            for u in range(t + 1, 8):
                lead = jnp.broadcast_to(cols[u][0][t : t + 1, :], (8, 128))
                cols[u] = [c - fh * lead for c, fh in zip(cols[u], f)]
            lead = jnp.broadcast_to(rows[g][t : t + 1, :], (8, 128))
            for h in range(count):
                rows[g + h] = rows[g + h] - f[h] * lead
            yield
        scale = lax.rsqrt(pivots)
        scale = scale * (1.5 - 0.5 * pivots * scale * scale)
        rows[g] = rows[g] * scale


def load_block(s_ref, at):
    base = (at // 128) * 128
    off = at - base
    other = 64 - off
    width = min(128, s_ref.shape[1] - base)
    lane = lax.broadcasted_iota(jnp.int32, (8, 128), 1)
    row = lax.broadcasted_iota(jnp.int32, (8, 128), 0)
    rows = []
    for g in range(8):
        piece = s_ref[at + 8 * g : at + 8 * g + 8, base : base + width]
        if width < 128:
            piece = jnp.concatenate([piece, jnp.zeros((8, 128 - width), jnp.float32)], axis=1)
        eye = (lane == row + (8 * g + other)).astype(jnp.float32)
        rows.append(jnp.where((lane >= off) & (lane < off + 64), piece, eye))
    return rows, off, other


def apply_block(rows, other, s_ref, pt_ref, qt_ref, at):
    n = s_ref.shape[0]
    inv = jnp.concatenate(rows, axis=0)
    if other:
        inv = pltpu.roll(inv, 64, axis=1)
    inv = inv[:, :64]
    wp = mm(inv, pt_ref[at : at + 64, :])
    qt_ref[at : at + 64, :] = wp
    if at + 64 < n:
        start = ((at + 64) // 128) * 128
        ws = mm(inv, s_ref[at : at + 64, start:])
        s_ref[start:, start:] = s_ref[start:, start:] - mm(ws, ws, 0, 0)
        pt_ref[start:, :] = pt_ref[start:, :] - mm(ws, wp, 0, 0)


def refresh_kernel(
    member_ref, factor_ref, gl_ref, bl_ref, gr_ref, br_ref, tile_ref, fm_ref, sm_ref,
    qlt_ref, qrt_ref, m_ref, v_ref, turned_ref,
    sl_ref, pl_ref, sr_ref, pr_ref,
):
    for g_ref, b_ref, s_ref, p_ref in (
        (gl_ref, bl_ref, sl_ref, pl_ref),
        (gr_ref, br_ref, sr_ref, pr_ref),
    ):
        pt = mm(b_ref[...], g_ref[...], 0, 0)
        p_ref[...] = pt
        s_ref[...] = mm(pt, pt, 1, 1)
    for step in range(LB // NB):
        at = step * NB
        jobs = []
        for s_ref, p_ref, q_ref in ((sl_ref, pl_ref, qlt_ref), (sr_ref, pr_ref, qrt_ref)):
            if at < s_ref.shape[0]:
                rows, off, other = load_block(s_ref, at)
                jobs.append((rows, other, s_ref, p_ref, q_ref, eliminate(rows, off)))
        live = [j[5] for j in jobs]
        while live:
            live = [g for g in live if next(g, 1) is None]
        for rows, other, s_ref, p_ref, q_ref, _ in jobs:
            apply_block(rows, other, s_ref, p_ref, q_ref, at)
    start = pl.multiple_of(member_ref[0] * 40, 8)
    own = qlt_ref[pl.ds(start, 40), :]
    rotated = mm(mm(own, tile_ref[...]) * factor_ref[0], qrt_ref[...], 1, 1)
    moment = beta_first * fm_ref[...] + (1.0 - beta_first) * rotated
    second = beta_second * sm_ref[...] + (1.0 - beta_second) * rotated * rotated
    direction = moment / first_bias / (jnp.sqrt(second / second_bias) + 1e-08)
    m_ref[...] = moment
    v_ref[...] = second
    turned_ref[...] = mm(direction, qrt_ref[...])


def refresh(member, factor, gl, bl, gr, br, tile, fm, sm):
    f32 = jnp.float32
    smem = pl.BlockSpec(memory_space=pltpu.SMEM)
    vmem = pl.BlockSpec(memory_space=pltpu.VMEM)
    return pl.pallas_call(
        refresh_kernel,
        out_shape=(
            jax.ShapeDtypeStruct((LB, LB), f32),
            jax.ShapeDtypeStruct((RB, RB), f32),
            jax.ShapeDtypeStruct((40, RB), f32),
            jax.ShapeDtypeStruct((40, RB), f32),
            jax.ShapeDtypeStruct((40, RB), f32),
        ),
        in_specs=[smem, smem] + [vmem] * 7,
        out_specs=(vmem,) * 5,
        scratch_shapes=[
            pltpu.VMEM((LB, LB), f32),
            pltpu.VMEM((LB, LB), f32),
            pltpu.VMEM((RB, RB), f32),
            pltpu.VMEM((RB, RB), f32),
        ],
        compiler_params=pltpu.CompilerParams(vmem_limit_bytes=24 * 2**20),
        cost_estimate=pl.CostEstimate(
            flops=40_000_000_000, bytes_accessed=4_000_000, transcendentals=0
        ),
        name="refresh",
    )(member, factor, gl, bl, gr, br, tile, fm, sm)


def place_kernel(y_ref, *refs):
    halves, out_ref = refs[:-1], refs[-1]
    y = y_ref[0]
    for n, (shift, first, count) in enumerate(PLACES):
        source = lax.rem(y + shift + 8, 8)
        at = pl.multiple_of(source * 160 + first, 16)
        out_ref[pl.ds(at, count), :] = halves[n][...].astype(jnp.bfloat16)


PLACES = (
    (0, 0, 160), (-1, 0, 160), (-2, 0, 160), (-3, 0, 160), (-4, 0, 80),
    (1, 0, 160), (2, 0, 160), (3, 0, 160), (4, 80, 80),
)


def place(y, halves):
    vmem = pl.BlockSpec(memory_space=pltpu.VMEM)
    return pl.pallas_call(
        place_kernel,
        out_shape=jax.ShapeDtypeStruct((1280, RB), jnp.bfloat16),
        in_specs=[pl.BlockSpec(memory_space=pltpu.SMEM)] + [vmem] * len(halves),
        out_specs=vmem,
        compiler_params=pltpu.CompilerParams(vmem_limit_bytes=16 * 2**20),
        name="place",
    )(y, *halves)


def gather_all(x, axes, count):
    copies = jnp.broadcast_to(x[None], (count,) + x.shape)
    return lax.all_to_all(copies, axes, 0, 0, tiled=True)


def shift_perm(size, by):
    return [(s, (s + by) % size) for s in range(size)]


def shards(
    pseudo_grads, left_gram, right_gram, left_basis, right_basis, first_moment, second_moment
):
    k = lax.axis_index("yk")
    x = lax.axis_index("x")
    y = lax.axis_index(("yk", "y2"))
    member = lax.axis_index(MEMBERS)

    held = jnp.concatenate([left_gram, left_basis], axis=0)
    moved = jnp.where(x == k, held, 0.0)
    for by in range(1, 4):
        moved = moved + lax.ppermute(
            held, ("yk", "x"), [(b * 4 + b, b * 4 + (b + by) % 4) for b in range(4)]
        )
    gram_k, basis_k = moved[0], moved[1]

    pieces = pseudo_grads[0].astype(jnp.float32).reshape(32, 40, RB)
    arrived = lax.all_to_all(pieces, REP, 0, 0, tiled=True)
    own = jnp.sum(arrived, axis=0) * (1.0 / 32.0)

    tile = gather_all(own, MEMBERS, 8).reshape(LB, RB)
    squares = jnp.full((8, RB), jnp.sum(tile * tile), jnp.float32)
    tiles = [tile] + [lax.ppermute(tile, "x", shift_perm(4, by)) for by in range(1, 4)]
    row_squares = squares
    for by in range(1, 4):
        row_squares = row_squares + lax.ppermute(squares, "x", shift_perm(4, by))

    right_part = mm(tile, tile, 0, 0).reshape(16, 16, RB)
    right_own = jnp.sum(lax.all_to_all(right_part, RIGHT_GROUP, 0, 0, tiled=True), axis=0)
    right_all = gather_all(jnp.concatenate([right_own, row_squares], axis=0), RIGHT_GROUP, 16)
    right_raw = right_all[:, :16].reshape(RB, RB)
    total = jnp.sum(right_all[:, 16, 0])
    factor = clip_ratio * math.sqrt(D * KV) / (jnp.sqrt(total) + 1e-06)
    weight = (1.0 - beta_gram) * factor * factor
    right_new = beta_gram * right_gram[0] + weight * right_raw

    left_raw = mm(tiles[0], tiles[0], 1, 1)
    for t in tiles[1:]:
        left_raw = left_raw + mm(t, t, 1, 1)
    left_new = beta_gram * gram_k + weight * left_raw
    swap = [(a * 4 + b, b * 4 + a) for a in range(4) for b in range(4)]
    left_new_out = lax.ppermute(left_new, ("yk", "x"), swap)

    qlt, qrt, moment, second, turned = refresh(
        member.astype(jnp.int32).reshape(1), factor.reshape(1), left_new, basis_k,
        right_new, right_basis[0], tile, first_moment, second_moment,
    )
    left_basis_out = lax.ppermute(qlt, ("yk", "x"), swap).T

    whole_turned = gather_all(turned, MEMBERS, 8).reshape(LB, RB)
    half = lax.dynamic_slice_in_dim(qlt, lax.axis_index("y2") * 160, 160, 1)
    mine = mm(half, whole_turned, 0, 0)
    ring = ("yk", "y2")
    right, left = [mine], [mine]
    for step in range(1, 4):
        right.append(lax.ppermute(right[-1], ring, shift_perm(8, 1)))
        left.append(lax.ppermute(left[-1], ring, shift_perm(8, -1)))
    right.append(lax.ppermute(right[-1][:80], ring, shift_perm(8, 1)))
    left.append(lax.ppermute(left[-1][80:], ring, shift_perm(8, -1)))
    update = place(y.astype(jnp.int32).reshape(1), right + left[1:])
    return (
        update, left_new_out[None], left_basis_out[None], right_new[None], qrt.T[None],
        moment, second,
    )


def solution(mesh):
    fine = Mesh(
        mesh.devices.reshape(4, 2, 4, 2, 2, 4), ("yk", "y2", "zh", "zl", "core", "x")
    )
    left = P(ROW + ("x",), None, None)
    right = P("x", None, None)
    moments = P(ROW + REP, "x")
    return jax.shard_map(
        shards,
        mesh=fine,
        in_specs=(P(REP, ROW, "x"), left, right, left, right, moments, moments),
        out_specs=(P(ROW, "x"), left, left, right, right, moments, moments),
        check_vma=False,
    )
```

```python
import math

import jax
import jax.numpy as jnp
from jax import lax
from jax.experimental import pallas as pl
from jax.experimental.pallas import tpu as pltpu
from jax.sharding import Mesh, PartitionSpec as P

D = 5120
KV = 1024
LB = 320
RB = 256
NB = 64

highest = lax.Precision.HIGHEST
beta_gram = 0.95
beta_first = 0.95
beta_second = 0.95
first_bias = 1.0 - 0.95**4
second_bias = 1.0 - 0.95**4
clip_ratio = 0.5

REP = ("yk", "y2", "zh")
ROW = ("zl", "core")
MEMBERS = ("y2", "zh")
RIGHT_GROUP = ("yk", "zl", "core")


def mm(a, b, ca=1, cb=0):
    return lax.dot_general(
        a, b, (((ca,), (cb,)), ((), ())), precision=highest, preferred_element_type=jnp.float32
    )


def eliminate(rows, off):
    row_id = lax.broadcasted_iota(jnp.int32, (8, 128), 0)
    for g in range(8):
        count = 8 - g
        cols = [
            [
                jnp.broadcast_to(rows[g + h][:, off + 8 * g + t : off + 8 * g + t + 1], (8, 128))
                for h in range(count)
            ]
            for t in range(8)
        ]
        pivots = jnp.ones((8, 128), jnp.float32)
        for t in range(8):
            pivot = jnp.broadcast_to(cols[t][0][t : t + 1, :], (8, 128))
            inv = 1.0 / pivot
            pivots = jnp.where(row_id == t, pivot, pivots)
            f = [c * inv for c in cols[t]]
            f[0] = jnp.where(row_id > t, f[0], 0.0)
            for u in range(t + 1, 8):
                lead = jnp.broadcast_to(cols[u][0][t : t + 1, :], (8, 128))
                cols[u] = [c - fh * lead for c, fh in zip(cols[u], f)]
            lead = jnp.broadcast_to(rows[g][t : t + 1, :], (8, 128))
            for h in range(count):
                rows[g + h] = rows[g + h] - f[h] * lead
            yield
        scale = lax.rsqrt(pivots)
        scale = scale * (1.5 - 0.5 * pivots * scale * scale)
        rows[g] = rows[g] * scale


def load_block(s_ref, at):
    base = (at // 128) * 128
    off = at - base
    other = 64 - off
    width = min(128, s_ref.shape[1] - base)
    lane = lax.broadcasted_iota(jnp.int32, (8, 128), 1)
    row = lax.broadcasted_iota(jnp.int32, (8, 128), 0)
    rows = []
    for g in range(8):
        piece = s_ref[at + 8 * g : at + 8 * g + 8, base : base + width]
        if width < 128:
            piece = jnp.concatenate([piece, jnp.zeros((8, 128 - width), jnp.float32)], axis=1)
        eye = (lane == row + (8 * g + other)).astype(jnp.float32)
        rows.append(jnp.where((lane >= off) & (lane < off + 64), piece, eye))
    return rows, off, other


def apply_block(rows, other, s_ref, pt_ref, qt_ref, at):
    n = s_ref.shape[0]
    inv = jnp.concatenate(rows, axis=0)
    if other:
        inv = pltpu.roll(inv, 64, axis=1)
    inv = inv[:, :64]
    wp = mm(inv, pt_ref[at : at + 64, :])
    qt_ref[at : at + 64, :] = wp
    if at + 64 < n:
        start = ((at + 64) // 128) * 128
        ws = mm(inv, s_ref[at : at + 64, start:])
        s_ref[start:, start:] = s_ref[start:, start:] - mm(ws, ws, 0, 0)
        pt_ref[start:, :] = pt_ref[start:, :] - mm(ws, wp, 0, 0)


def factorize(jobs):
    for gram, basis, s_ref, p_ref, _ in jobs:
        pt = mm(basis, gram, 0, 0)
        p_ref[...] = pt
        s_ref[...] = mm(pt, pt, 1, 1)
    for step in range(LB // NB):
        at = step * NB
        blocks = []
        for _, _, s_ref, p_ref, qt_ref in jobs:
            if at < s_ref.shape[0]:
                rows, off, other = load_block(s_ref, at)
                blocks.append((rows, other, s_ref, p_ref, qt_ref, eliminate(rows, off)))
        live = [b[5] for b in blocks]
        while live:
            live = [g for g in live if next(g, 1) is None]
        for rows, other, s_ref, p_ref, qt_ref, _ in blocks:
            apply_block(rows, other, s_ref, p_ref, qt_ref, at)


def refresh_kernel(
    member_ref, left_raw_ref, gl_ref, bl_ref, right_raw_ref, gr_ref, br_ref, tile_ref, moments_ref,
    gr_out_ref, qr_out_ref, m_ref, v_ref, u_ref, factor_ref,
    sl_ref, pl_ref, qlt_ref, sr_ref, pr_ref, qrt_ref, ms_ref, vs_ref,
):
    packed = right_raw_ref[...]
    row = lax.broadcasted_iota(jnp.int32, (RB, RB), 0)
    col = lax.broadcasted_iota(jnp.int32, (RB, RB), 1)
    slot = (row % 16 == 0) & (col == row + 1)
    total = jnp.sum(jnp.where(slot, packed, 0.0), keepdims=True)
    right_raw = jnp.where(slot, packed.T, packed)
    factor = clip_ratio * math.sqrt(D * KV) / (jnp.sqrt(total) + 1e-06)
    factor_ref[...] = jnp.broadcast_to(factor, factor_ref.shape)
    weight = (1.0 - beta_gram) * factor * factor
    right_new = beta_gram * gr_ref[...] + weight * right_raw
    gr_out_ref[...] = right_new
    left_new = beta_gram * gl_ref[...] + weight * left_raw_ref[...]
    factorize(
        [
            (left_new, bl_ref[...], sl_ref, pl_ref, qlt_ref),
            (right_new, br_ref[...], sr_ref, pr_ref, qrt_ref),
        ]
    )
    qrt = qrt_ref[...]
    qr_out_ref[...] = qrt.T
    rotated = mm(mm(qlt_ref[...], tile_ref[...]) * factor, qrt, 1, 1)
    moment = beta_first * moments_ref[:, :40, :].reshape(LB, RB) + (1.0 - beta_first) * rotated
    second = beta_second * moments_ref[:, 40:, :].reshape(LB, RB)
    second = second + (1.0 - beta_second) * rotated * rotated
    ms_ref[...] = moment
    vs_ref[...] = second
    direction = moment / first_bias / (jnp.sqrt(second / second_bias) + 1e-08)
    u_ref[...] = mm(qlt_ref[...], mm(direction, qrt), 0, 0)
    own = pl.ds(pl.multiple_of(member_ref[0] * 40, 8), 40)
    m_ref[...] = ms_ref[own, :]
    v_ref[...] = vs_ref[own, :]


def shape_of(*dims):
    return jax.ShapeDtypeStruct(dims, jnp.float32)


def whole():
    return pl.BlockSpec(memory_space=pltpu.VMEM)


def refresh(member, left_raw, gl, bl, right_raw, gr, br, tile, moments):
    f32 = jnp.float32
    return pl.pallas_call(
        refresh_kernel,
        out_shape=(
            shape_of(RB, RB), shape_of(RB, RB), shape_of(40, RB), shape_of(40, RB),
            shape_of(LB, RB), shape_of(8, 128),
        ),
        in_specs=[pl.BlockSpec(memory_space=pltpu.SMEM)] + [whole()] * 8,
        out_specs=(whole(),) * 6,
        scratch_shapes=[pltpu.VMEM((LB, LB), f32)] * 3
        + [pltpu.VMEM((RB, RB), f32)] * 3
        + [pltpu.VMEM((LB, RB), f32)] * 2,
        compiler_params=pltpu.CompilerParams(vmem_limit_bytes=24 * 2**20),
        cost_estimate=pl.CostEstimate(
            flops=25_000_000_000, bytes_accessed=4_000_000, transcendentals=0
        ),
        name="refresh",
    )(member, left_raw, gl, bl, right_raw, gr, br, tile, moments)


def held_kernel(factor_ref, raw_ref, g_ref, b_ref, g_out_ref, q_out_ref, s_ref, p_ref, qt_ref):
    factor = factor_ref[:1, :1]
    gram = beta_gram * g_ref[...] + (1.0 - beta_gram) * factor * factor * raw_ref[...]
    g_out_ref[...] = gram
    factorize([(gram, b_ref[...], s_ref, p_ref, qt_ref)])
    q_out_ref[...] = qt_ref[...].T


def refresh_held(factor, raw, gram, basis):
    f32 = jnp.float32
    return pl.pallas_call(
        held_kernel,
        out_shape=(shape_of(LB, LB), shape_of(LB, LB)),
        in_specs=[whole()] * 4,
        out_specs=(whole(),) * 2,
        scratch_shapes=[pltpu.VMEM((LB, LB), f32)] * 3,
        compiler_params=pltpu.CompilerParams(vmem_limit_bytes=24 * 2**20),
        cost_estimate=pl.CostEstimate(
            flops=18_000_000_000, bytes_accessed=2_000_000, transcendentals=0
        ),
        name="refresh_held",
    )(factor, raw, gram, basis)


PLACES = ((0, 0, 320), (-1, 0, 320), (1, 0, 320), (2, 0, 160), (2, 160, 160))


def place_kernel(k_ref, *refs):
    parts, out_ref, rounded_ref, sems = refs[:-3], refs[-3], refs[-2], refs[-1]
    copies = []
    for n, (shift, first, count) in enumerate(PLACES):
        source = lax.rem(k_ref[0] + shift + 4, 4)
        at = pl.ds(pl.multiple_of(source * LB + first, 16), count)
        rounded_ref[at, :] = parts[n][...].astype(jnp.bfloat16)
        copies.append(pltpu.make_async_copy(rounded_ref.at[at], out_ref.at[at], sems.at[n]))
        copies[-1].start()
    for copy in copies:
        copy.wait()


def place(k, parts):
    return pl.pallas_call(
        place_kernel,
        out_shape=jax.ShapeDtypeStruct((4 * LB, RB), jnp.bfloat16),
        in_specs=[pl.BlockSpec(memory_space=pltpu.SMEM)] + [whole()] * len(parts),
        out_specs=pl.BlockSpec(memory_space=pl.ANY),
        scratch_shapes=[
            pltpu.VMEM((4 * LB, RB), jnp.bfloat16),
            pltpu.SemaphoreType.DMA((len(PLACES),)),
        ],
        compiler_params=pltpu.CompilerParams(vmem_limit_bytes=16 * 2**20),
        name="place",
    )(k, *parts)


def gather_all(x, axes, count):
    copies = jnp.broadcast_to(x[None], (count,) + x.shape)
    return lax.all_to_all(copies, axes, 0, 0, tiled=True)


def shift_perm(size, by):
    return [(s, (s + by) % size) for s in range(size)]


def shards(
    pseudo_grads, left_gram, right_gram, left_basis, right_basis, first_moment, second_moment
):
    k = lax.axis_index("yk")
    x = lax.axis_index("x")
    member = lax.axis_index(MEMBERS)

    moments = lax.all_gather(
        jnp.concatenate([first_moment, second_moment], axis=0), MEMBERS, axis=0, tiled=False
    )

    held = jnp.concatenate([left_gram, left_basis], axis=0)
    moved = jnp.where(x == k, held, 0.0)
    for by in range(1, 4):
        moved = moved + lax.ppermute(
            held, ("yk", "x"), [(b * 4 + b, b * 4 + (b + by) % 4) for b in range(4)]
        )

    pieces = pseudo_grads[0].astype(jnp.float32).reshape(32, 40, RB)
    arrived = lax.all_to_all(pieces, REP, 0, 0, tiled=True)
    own = jnp.sum(arrived, axis=0) * (1.0 / 32.0)

    tile = gather_all(own, MEMBERS, 8).reshape(LB, RB)
    right_part = mm(tile, tile, 0, 0).reshape(16, 16, RB)
    right_own = jnp.sum(lax.all_to_all(right_part, RIGHT_GROUP, 0, 0, tiled=True), axis=0)
    tiles = [tile] + [lax.ppermute(tile, "x", shift_perm(4, by)) for by in range(1, 4)]
    squares = sum(jnp.sum(t * t) for t in tiles)

    group = lax.axis_index(RIGHT_GROUP)
    row = lax.broadcasted_iota(jnp.int32, (16, RB), 0)
    col = lax.broadcasted_iota(jnp.int32, (16, RB), 1)
    packed = jnp.where((row == 0) & (col == 16 * group + 1), squares, right_own)
    right_raw = gather_all(packed, RIGHT_GROUP, 16).reshape(RB, RB)

    left_raw = mm(tiles[0], tiles[0], 1, 1)
    for t in tiles[1:]:
        left_raw = left_raw + mm(t, t, 1, 1)
    swap = [(a * 4 + b, b * 4 + a) for a in range(4) for b in range(4)]
    held_raw = lax.ppermute(left_raw, ("yk", "x"), swap)

    right_new, right_basis_new, moment, second, turned, factor = refresh(
        member.astype(jnp.int32).reshape(1), left_raw, moved[0], moved[1], right_raw,
        right_gram[0], right_basis[0], tile, moments,
    )

    before = lax.ppermute(turned, "yk", shift_perm(4, 1))
    after = lax.ppermute(turned, "yk", shift_perm(4, -1))
    left_new, left_basis_new = refresh_held(factor, held_raw, left_gram[0], left_basis[0])
    before, after, left_new, left_basis_new = lax.optimization_barrier(
        (before, after, left_new, left_basis_new)
    )
    upper = lax.ppermute(before[:160], "yk", shift_perm(4, 1))
    lower = lax.ppermute(after[160:], "yk", shift_perm(4, -1))
    update = place(k.astype(jnp.int32).reshape(1), [turned, before, after, upper, lower])
    return (
        update, left_new[None], left_basis_new[None], right_new[None], right_basis_new[None],
        moment, second,
    )


def solution(mesh):
    fine = Mesh(
        mesh.devices.reshape(4, 2, 4, 2, 2, 4), ("yk", "y2", "zh", "zl", "core", "x")
    )
    left = P(ROW + ("x",), None, None)
    right = P("x", None, None)
    moments = P(ROW + REP, "x")
    return jax.shard_map(
        shards,
        mesh=fine,
        in_specs=(P(REP, ROW, "x"), left, right, left, right, moments, moments),
        out_specs=(P(ROW, "x"), left, left, right, right, moments, moments),
        check_vma=False,
    )
```

```python
import math

import jax
import jax.numpy as jnp
from jax import lax
from jax.experimental import pallas as pl
from jax.experimental.pallas import tpu as pltpu
from jax.sharding import Mesh, PartitionSpec as P

D = 5120
KV = 1024
LB = 320
RB = 256
NB = 64

highest = lax.Precision.HIGHEST
beta_gram = 0.95
beta_first = 0.95
beta_second = 0.95
first_bias = 1.0 - 0.95**4
second_bias = 1.0 - 0.95**4
clip_ratio = 0.5

REP = ("yk", "y2", "zh")
ROW = ("zl", "core")
MEMBERS = ("y2", "zh")
RIGHT_GROUP = ("yk", "zl", "core")


def mm(a, b, ca=1, cb=0):
    return lax.dot_general(
        a, b, (((ca,), (cb,)), ((), ())), precision=highest, preferred_element_type=jnp.float32
    )


def eliminate(rows, off):
    row_id = lax.broadcasted_iota(jnp.int32, (8, 128), 0)
    for g in range(8):
        count = 8 - g
        cols = [
            [
                jnp.broadcast_to(rows[g + h][:, off + 8 * g + t : off + 8 * g + t + 1], (8, 128))
                for h in range(count)
            ]
            for t in range(8)
        ]
        pivots = jnp.ones((8, 128), jnp.float32)
        for t in range(8):
            pivot = jnp.broadcast_to(cols[t][0][t : t + 1, :], (8, 128))
            inv = 1.0 / pivot
            pivots = jnp.where(row_id == t, pivot, pivots)
            f = [c * inv for c in cols[t]]
            f[0] = jnp.where(row_id > t, f[0], 0.0)
            for u in range(t + 1, 8):
                lead = jnp.broadcast_to(cols[u][0][t : t + 1, :], (8, 128))
                cols[u] = [c - fh * lead for c, fh in zip(cols[u], f)]
            lead = jnp.broadcast_to(rows[g][t : t + 1, :], (8, 128))
            for h in range(count):
                rows[g + h] = rows[g + h] - f[h] * lead
            yield
        scale = lax.rsqrt(pivots)
        scale = scale * (1.5 - 0.5 * pivots * scale * scale)
        rows[g] = rows[g] * scale


def load_block(s_ref, at):
    base = (at // 128) * 128
    off = at - base
    other = 64 - off
    width = min(128, s_ref.shape[1] - base)
    lane = lax.broadcasted_iota(jnp.int32, (8, 128), 1)
    row = lax.broadcasted_iota(jnp.int32, (8, 128), 0)
    rows = []
    for g in range(8):
        piece = s_ref[at + 8 * g : at + 8 * g + 8, base : base + width]
        if width < 128:
            piece = jnp.concatenate([piece, jnp.zeros((8, 128 - width), jnp.float32)], axis=1)
        eye = (lane == row + (8 * g + other)).astype(jnp.float32)
        rows.append(jnp.where((lane >= off) & (lane < off + 64), piece, eye))
    return rows, off, other


def apply_block(rows, other, s_ref, pt_ref, qt_ref, at):
    n = s_ref.shape[0]
    inv = jnp.concatenate(rows, axis=0)
    if other:
        inv = pltpu.roll(inv, 64, axis=1)
    inv = inv[:, :64]
    wp = mm(inv, pt_ref[at : at + 64, :])
    qt_ref[at : at + 64, :] = wp
    if at + 64 < n:
        start = ((at + 64) // 128) * 128
        ws = mm(inv, s_ref[at : at + 64, start:])
        s_ref[start:, start:] = s_ref[start:, start:] - mm(ws, ws, 0, 0)
        pt_ref[start:, :] = pt_ref[start:, :] - mm(ws, wp, 0, 0)


def factorize(jobs):
    for gram, basis, s_ref, p_ref, _ in jobs:
        pt = mm(basis, gram, 0, 0)
        p_ref[...] = pt
        s_ref[...] = mm(pt, pt, 1, 1)
    for step in range(LB // NB):
        at = step * NB
        blocks = []
        for _, _, s_ref, p_ref, qt_ref in jobs:
            if at < s_ref.shape[0]:
                rows, off, other = load_block(s_ref, at)
                blocks.append((rows, other, s_ref, p_ref, qt_ref, eliminate(rows, off)))
        live = [b[5] for b in blocks]
        while live:
            live = [g for g in live if next(g, 1) is None]
        for rows, other, s_ref, p_ref, qt_ref, _ in blocks:
            apply_block(rows, other, s_ref, p_ref, qt_ref, at)


def slots(shape, row_at, col_at):
    row = lax.broadcasted_iota(jnp.int32, shape, 0)
    col = lax.broadcasted_iota(jnp.int32, shape, 1)
    return (row % 16 == row_at) & (col == row + col_at)


def refresh_kernel(
    place_ref, left_raw_ref, gl_ref, bl_ref, right_raw_ref, gr_ref, br_ref, tile_ref, squares_ref,
    mine_ref, other_ref,
    gr_out_ref, qr_out_ref, m_ref, v_ref, u_ref, factor_ref,
    sl_ref, pl_ref, qlt_ref, sr_ref, pr_ref, qrt_ref, ms_ref, vs_ref,
):
    y2, zh = place_ref[0], place_ref[1]
    for src_ref, pair in ((mine_ref, y2), (other_ref, 1 - y2)):
        for n, shift in enumerate((0, -1, 1, 2)):
            at = pl.multiple_of(40 * (4 * pair + lax.rem(zh + shift + 4, 4)), 8)
            ms_ref[pl.ds(at, 40), :] = src_ref[80 * n : 80 * n + 40, :]
            vs_ref[pl.ds(at, 40), :] = src_ref[80 * n + 40 : 80 * n + 80, :]
    packed = right_raw_ref[...]
    slot = slots((RB, RB), 0, 1)
    right_raw = jnp.where(slot, packed.T, packed)
    total = (squares_ref[0] + squares_ref[1] + squares_ref[2] + squares_ref[3])[:1, :1]
    factor = clip_ratio * math.sqrt(D * KV) / (jnp.sqrt(total) + 1e-06)
    factor_ref[...] = jnp.broadcast_to(factor, factor_ref.shape)
    weight = (1.0 - beta_gram) * factor * factor
    right_new = beta_gram * gr_ref[...] + weight * right_raw
    gr_out_ref[...] = right_new
    left_new = beta_gram * gl_ref[...] + weight * left_raw_ref[...]
    factorize(
        [
            (left_new, bl_ref[...], sl_ref, pl_ref, qlt_ref),
            (right_new, br_ref[...], sr_ref, pr_ref, qrt_ref),
        ]
    )
    qrt = qrt_ref[...]
    qr_out_ref[...] = qrt.T
    rotated = mm(mm(qlt_ref[...], tile_ref[...]) * factor, qrt, 1, 1)
    moment = beta_first * ms_ref[...] + (1.0 - beta_first) * rotated
    second = beta_second * vs_ref[...] + (1.0 - beta_second) * rotated * rotated
    ms_ref[...] = moment
    vs_ref[...] = second
    direction = moment / first_bias / (jnp.sqrt(second / second_bias) + 1e-08)
    u_ref[...] = mm(qlt_ref[...], mm(direction, qrt), 0, 0)
    own = pl.ds(pl.multiple_of(40 * (4 * y2 + zh), 8), 40)
    m_ref[...] = ms_ref[own, :]
    v_ref[...] = vs_ref[own, :]


def shape_of(*dims):
    return jax.ShapeDtypeStruct(dims, jnp.float32)


def whole():
    return pl.BlockSpec(memory_space=pltpu.VMEM)


def refresh(spot, left_raw, gl, bl, right_raw, gr, br, tile, squares, mine, other):
    f32 = jnp.float32
    return pl.pallas_call(
        refresh_kernel,
        out_shape=(
            shape_of(RB, RB), shape_of(RB, RB), shape_of(40, RB), shape_of(40, RB),
            shape_of(LB, RB), shape_of(8, 128),
        ),
        in_specs=[pl.BlockSpec(memory_space=pltpu.SMEM)] + [whole()] * 10,
        out_specs=(whole(),) * 6,
        scratch_shapes=[pltpu.VMEM((LB, LB), f32)] * 3
        + [pltpu.VMEM((RB, RB), f32)] * 3
        + [pltpu.VMEM((LB, RB), f32)] * 2,
        compiler_params=pltpu.CompilerParams(vmem_limit_bytes=24 * 2**20),
        cost_estimate=pl.CostEstimate(
            flops=25_000_000_000, bytes_accessed=4_000_000, transcendentals=0
        ),
        name="refresh",
    )(spot, left_raw, gl, bl, right_raw, gr, br, tile, squares, mine, other)


def held_kernel(factor_ref, raw_ref, g_ref, b_ref, g_out_ref, q_out_ref, s_ref, p_ref, qt_ref):
    factor = factor_ref[:1, :1]
    gram = beta_gram * g_ref[...] + (1.0 - beta_gram) * factor * factor * raw_ref[...]
    g_out_ref[...] = gram
    factorize([(gram, b_ref[...], s_ref, p_ref, qt_ref)])
    q_out_ref[...] = qt_ref[...].T


def refresh_held(factor, raw, gram, basis):
    f32 = jnp.float32
    return pl.pallas_call(
        held_kernel,
        out_shape=(shape_of(LB, LB), shape_of(LB, LB)),
        in_specs=[whole()] * 4,
        out_specs=(whole(),) * 2,
        scratch_shapes=[pltpu.VMEM((LB, LB), f32)] * 3,
        compiler_params=pltpu.CompilerParams(vmem_limit_bytes=24 * 2**20),
        cost_estimate=pl.CostEstimate(
            flops=18_000_000_000, bytes_accessed=2_000_000, transcendentals=0
        ),
        name="refresh_held",
    )(factor, raw, gram, basis)


def own_sum_kernel(arrived_ref, out_ref):
    total = arrived_ref[0]
    for r in range(1, 32):
        total = total + arrived_ref[r]
    total = total * (1.0 / 32.0)
    for n in range(8):
        out_ref[n] = total


def right_part_kernel(tile_ref, out_ref):
    tile = tile_ref[...]
    squares = jnp.sum(tile * tile, keepdims=True)
    out_ref[...] = jnp.where(slots((RB, RB), 0, 1), squares, mm(tile, tile, 0, 0))


def right_sum_kernel(group_ref, parts_ref, out_ref, squares_ref):
    total = parts_ref[0]
    for r in range(1, 16):
        total = total + parts_ref[r]
    for n in range(16):
        out_ref[n] = total
    slot = slots((16, RB), 0, 16 * group_ref[0] + 1)
    squares = jnp.sum(jnp.where(slot, total, 0.0), keepdims=True)
    squares_ref[...] = jnp.broadcast_to(squares, squares_ref.shape)


def left_gram_kernel(tiles_ref, out_ref):
    total = mm(tiles_ref[0], tiles_ref[0], 1, 1)
    for n in range(1, 4):
        total = total + mm(tiles_ref[n], tiles_ref[n], 1, 1)
    out_ref[...] = total


def small(kernel, name, out_shape, flops, *operands, scalars=0):
    specs = [pl.BlockSpec(memory_space=pltpu.SMEM)] * scalars
    specs = specs + [whole()] * (len(operands) - scalars)
    return pl.pallas_call(
        kernel,
        out_shape=out_shape,
        in_specs=specs,
        out_specs=jax.tree.map(lambda _: whole(), out_shape),
        compiler_params=pltpu.CompilerParams(vmem_limit_bytes=16 * 2**20),
        cost_estimate=pl.CostEstimate(flops=flops, bytes_accessed=1_000_000, transcendentals=0),
        name=name,
    )(*operands)


PLACES = ((0, 0, 320), (-1, 0, 320), (1, 0, 320), (2, 0, 160), (2, 160, 160))


def place_kernel(k_ref, *refs):
    parts, out_ref, rounded_ref, sems = refs[:-3], refs[-3], refs[-2], refs[-1]
    copies = []
    for n, (shift, first, count) in enumerate(PLACES):
        source = lax.rem(k_ref[0] + shift + 4, 4)
        at = pl.ds(pl.multiple_of(source * LB + first, 16), count)
        rounded_ref[at, :] = parts[n][...].astype(jnp.bfloat16)
        copies.append(pltpu.make_async_copy(rounded_ref.at[at], out_ref.at[at], sems.at[n]))
        copies[-1].start()
    for copy in copies:
        copy.wait()


def place(k, parts):
    return pl.pallas_call(
        place_kernel,
        out_shape=jax.ShapeDtypeStruct((4 * LB, RB), jnp.bfloat16),
        in_specs=[pl.BlockSpec(memory_space=pltpu.SMEM)] + [whole()] * len(parts),
        out_specs=pl.BlockSpec(memory_space=pl.ANY),
        scratch_shapes=[
            pltpu.VMEM((4 * LB, RB), jnp.bfloat16),
            pltpu.SemaphoreType.DMA((len(PLACES),)),
        ],
        compiler_params=pltpu.CompilerParams(vmem_limit_bytes=16 * 2**20),
        name="place",
    )(k, *parts)


def gather_all(x, axes, count):
    copies = jnp.broadcast_to(x[None], (count,) + x.shape)
    return lax.all_to_all(copies, axes, 0, 0, tiled=True)


def shift_perm(size, by):
    return [(s, (s + by) % size) for s in range(size)]


def shards(
    pseudo_grads, left_gram, right_gram, left_basis, right_basis, first_moment, second_moment
):
    k = lax.axis_index("yk")
    x = lax.axis_index("x")

    ours = jnp.concatenate([first_moment, second_moment], axis=0)
    prev = lax.ppermute(ours, "zh", shift_perm(4, 1))
    succ = lax.ppermute(ours, "zh", shift_perm(4, -1))
    far_first = lax.ppermute(prev[:40], "zh", shift_perm(4, 1))
    far_second = lax.ppermute(succ[40:], "zh", shift_perm(4, -1))
    mine = jnp.concatenate([ours, prev, succ, far_first, far_second], axis=0)
    other = lax.ppermute(mine, "y2", shift_perm(2, 1))

    held = jnp.concatenate([left_gram, left_basis], axis=0)
    moved = jnp.where(x == k, held, 0.0)
    for by in range(1, 4):
        moved = moved + lax.ppermute(
            held, ("yk", "x"), [(b * 4 + b, b * 4 + (b + by) % 4) for b in range(4)]
        )

    pieces = pseudo_grads[0].astype(jnp.float32).reshape(32, 40, RB)
    arrived = lax.all_to_all(pieces, REP, 0, 0, tiled=True)
    copies = small(own_sum_kernel, "own_sum", shape_of(8, 40, RB), 10**8, arrived)
    tile = lax.all_to_all(copies, MEMBERS, 0, 0, tiled=True).reshape(LB, RB)
    tile, mine, other = lax.optimization_barrier((tile, mine, other))

    right_part = small(right_part_kernel, "right_part", shape_of(RB, RB), 10**9, tile)
    parts = lax.all_to_all(right_part.reshape(16, 16, RB), RIGHT_GROUP, 0, 0, tiled=True)
    tiles = gather_all(tile, "x", 4)
    right_own, squares_own = small(
        right_sum_kernel, "right_sum", (shape_of(16, 16, RB), shape_of(4, 8, 128)), 10**8,
        lax.axis_index(RIGHT_GROUP).astype(jnp.int32).reshape(1), parts, scalars=1,
    )
    right_raw = lax.all_to_all(right_own, RIGHT_GROUP, 0, 0, tiled=True).reshape(RB, RB)
    squares = lax.all_to_all(squares_own, "x", 0, 0, tiled=True)
    left_raw = small(left_gram_kernel, "left_gram", shape_of(LB, LB), 2 * 10**9, tiles)
    swap = [(a * 4 + b, b * 4 + a) for a in range(4) for b in range(4)]
    held_raw = lax.ppermute(left_raw, ("yk", "x"), swap)

    right_new, right_basis_new, moment, second, turned, factor = refresh(
        jnp.stack([lax.axis_index("y2"), lax.axis_index("zh")]).astype(jnp.int32), left_raw,
        moved[0], moved[1], right_raw, right_gram[0], right_basis[0], tile, squares, mine, other,
    )

    before = lax.ppermute(turned, "yk", shift_perm(4, 1))
    after = lax.ppermute(turned, "yk", shift_perm(4, -1))
    left_new, left_basis_new = refresh_held(factor, held_raw, left_gram[0], left_basis[0])
    before, after, left_new, left_basis_new = lax.optimization_barrier(
        (before, after, left_new, left_basis_new)
    )
    upper = lax.ppermute(before[:160], "yk", shift_perm(4, 1))
    lower = lax.ppermute(after[160:], "yk", shift_perm(4, -1))
    update = place(k.astype(jnp.int32).reshape(1), [turned, before, after, upper, lower])
    return (
        update, left_new[None], left_basis_new[None], right_new[None], right_basis_new[None],
        moment, second,
    )


def solution(mesh):
    fine = Mesh(
        mesh.devices.reshape(4, 2, 4, 2, 2, 4), ("yk", "y2", "zh", "zl", "core", "x")
    )
    left = P(ROW + ("x",), None, None)
    right = P("x", None, None)
    moments = P(ROW + REP, "x")
    return jax.shard_map(
        shards,
        mesh=fine,
        in_specs=(P(REP, ROW, "x"), left, right, left, right, moments, moments),
        out_specs=(P(ROW, "x"), left, left, right, right, moments, moments),
        check_vma=False,
    )
```

```python
import math

import jax
import jax.numpy as jnp
from jax import lax
from jax.experimental import pallas as pl
from jax.experimental.pallas import tpu as pltpu
from jax.sharding import Mesh, PartitionSpec as P

D = 5120
KV = 1024
LB = 320
RB = 256
NB = 64

highest = lax.Precision.HIGHEST
beta_gram = 0.95
beta_first = 0.95
beta_second = 0.95
first_bias = 1.0 - 0.95**4
second_bias = 1.0 - 0.95**4
clip_ratio = 0.5

REP = ("yk", "y2", "zh")
ROW = ("zl", "core")
MEMBERS = ("y2", "zh")
RIGHT_GROUP = ("yk", "zl", "core")


def mm(a, b, ca=1, cb=0):
    return lax.dot_general(
        a, b, (((ca,), (cb,)), ((), ())), precision=highest, preferred_element_type=jnp.float32
    )


def eliminate(rows, off):
    row_id = lax.broadcasted_iota(jnp.int32, (8, 128), 0)
    for g in range(8):
        count = 8 - g
        cols = [
            [
                jnp.broadcast_to(rows[g + h][:, off + 8 * g + t : off + 8 * g + t + 1], (8, 128))
                for h in range(count)
            ]
            for t in range(8)
        ]
        pivots = jnp.ones((8, 128), jnp.float32)
        for t in range(8):
            pivot = jnp.broadcast_to(cols[t][0][t : t + 1, :], (8, 128))
            inv = 1.0 / pivot
            pivots = jnp.where(row_id == t, pivot, pivots)
            f = [c * inv for c in cols[t]]
            f[0] = jnp.where(row_id > t, f[0], 0.0)
            for u in range(t + 1, 8):
                lead = jnp.broadcast_to(cols[u][0][t : t + 1, :], (8, 128))
                cols[u] = [c - fh * lead for c, fh in zip(cols[u], f)]
            lead = jnp.broadcast_to(rows[g][t : t + 1, :], (8, 128))
            for h in range(count):
                rows[g + h] = rows[g + h] - f[h] * lead
            yield
        scale = lax.rsqrt(pivots)
        scale = scale * (1.5 - 0.5 * pivots * scale * scale)
        rows[g] = rows[g] * scale


def load_block(s_ref, at):
    base = (at // 128) * 128
    off = at - base
    other = 64 - off
    width = min(128, s_ref.shape[1] - base)
    lane = lax.broadcasted_iota(jnp.int32, (8, 128), 1)
    row = lax.broadcasted_iota(jnp.int32, (8, 128), 0)
    rows = []
    for g in range(8):
        piece = s_ref[at + 8 * g : at + 8 * g + 8, base : base + width]
        if width < 128:
            piece = jnp.concatenate([piece, jnp.zeros((8, 128 - width), jnp.float32)], axis=1)
        eye = (lane == row + (8 * g + other)).astype(jnp.float32)
        rows.append(jnp.where((lane >= off) & (lane < off + 64), piece, eye))
    return rows, off, other


def apply_block(rows, other, s_ref, pt_ref, qt_ref, at):
    n = s_ref.shape[0]
    inv = jnp.concatenate(rows, axis=0)
    if other:
        inv = pltpu.roll(inv, 64, axis=1)
    inv = inv[:, :64]
    wp = mm(inv, pt_ref[at : at + 64, :])
    qt_ref[at : at + 64, :] = wp
    if at + 64 < n:
        start = ((at + 64) // 128) * 128
        ws = mm(inv, s_ref[at : at + 64, start:])
        s_ref[start:, start:] = s_ref[start:, start:] - mm(ws, ws, 0, 0)
        pt_ref[start:, :] = pt_ref[start:, :] - mm(ws, wp, 0, 0)


def factorize(jobs):
    for gram, basis, s_ref, p_ref, _ in jobs:
        pt = mm(basis, gram, 0, 0)
        p_ref[...] = pt
        s_ref[...] = mm(pt, pt, 1, 1)
    for step in range(LB // NB):
        at = step * NB
        blocks = []
        for _, _, s_ref, p_ref, qt_ref in jobs:
            if at < s_ref.shape[0]:
                rows, off, other = load_block(s_ref, at)
                blocks.append((rows, other, s_ref, p_ref, qt_ref, eliminate(rows, off)))
        live = [b[5] for b in blocks]
        while live:
            live = [g for g in live if next(g, 1) is None]
        for rows, other, s_ref, p_ref, qt_ref, _ in blocks:
            apply_block(rows, other, s_ref, p_ref, qt_ref, at)


def slots(shape, row_at, col_at):
    row = lax.broadcasted_iota(jnp.int32, shape, 0)
    col = lax.broadcasted_iota(jnp.int32, shape, 1)
    return (row % 16 == row_at) & (col == row + col_at)


def refresh_kernel(
    place_ref, left_raw_ref, gl_ref, bl_ref, right_raw_ref, gr_ref, br_ref, tile_ref, sq0_ref, sq1_ref,
    sq2_ref, sq3_ref, mine_ref, other_ref,
    gr_out_ref, qr_out_ref, m_ref, v_ref, u_ref, factor_ref,
    sl_ref, pl_ref, qlt_ref, sr_ref, pr_ref, qrt_ref, ms_ref, vs_ref,
):
    y2, zh = place_ref[0], place_ref[1]
    for src_ref, pair in ((mine_ref, y2), (other_ref, 1 - y2)):
        for n, shift in enumerate((0, -1, -2, -3)):
            at = pl.multiple_of(40 * (4 * pair + lax.rem(zh + shift + 4, 4)), 8)
            ms_ref[pl.ds(at, 40), :] = src_ref[80 * n : 80 * n + 40, :]
            vs_ref[pl.ds(at, 40), :] = src_ref[80 * n + 40 : 80 * n + 80, :]
    packed = right_raw_ref[...]
    slot = slots((RB, RB), 0, 1)
    right_raw = jnp.where(slot, packed.T, packed)
    total = (sq0_ref[...] + sq1_ref[...] + (sq2_ref[...] + sq3_ref[...]))[:1, :1]
    factor = clip_ratio * math.sqrt(D * KV) / (jnp.sqrt(total) + 1e-06)
    factor_ref[...] = jnp.broadcast_to(factor, factor_ref.shape)
    weight = (1.0 - beta_gram) * factor * factor
    right_new = beta_gram * gr_ref[...] + weight * right_raw
    gr_out_ref[...] = right_new
    left_new = beta_gram * gl_ref[...] + weight * left_raw_ref[...]
    factorize(
        [
            (left_new, bl_ref[...], sl_ref, pl_ref, qlt_ref),
            (right_new, br_ref[...], sr_ref, pr_ref, qrt_ref),
        ]
    )
    qrt = qrt_ref[...]
    qr_out_ref[...] = qrt.T
    rotated = mm(mm(qlt_ref[...], tile_ref[...]) * factor, qrt, 1, 1)
    moment = beta_first * ms_ref[...] + (1.0 - beta_first) * rotated
    second = beta_second * vs_ref[...] + (1.0 - beta_second) * rotated * rotated
    ms_ref[...] = moment
    vs_ref[...] = second
    direction = moment / first_bias / (jnp.sqrt(second / second_bias) + 1e-08)
    u_ref[...] = mm(qlt_ref[...], mm(direction, qrt), 0, 0)
    own = pl.ds(pl.multiple_of(40 * (4 * y2 + zh), 8), 40)
    m_ref[...] = ms_ref[own, :]
    v_ref[...] = vs_ref[own, :]


def shape_of(*dims):
    return jax.ShapeDtypeStruct(dims, jnp.float32)


def whole():
    return pl.BlockSpec(memory_space=pltpu.VMEM)


def refresh(spot, left_raw, gl, bl, right_raw, gr, br, tile, squares, mine, other):
    f32 = jnp.float32
    return pl.pallas_call(
        refresh_kernel,
        out_shape=(
            shape_of(RB, RB), shape_of(RB, RB), shape_of(40, RB), shape_of(40, RB),
            shape_of(LB, RB), shape_of(8, 128),
        ),
        in_specs=[pl.BlockSpec(memory_space=pltpu.SMEM)] + [whole()] * 4 + [pl.BlockSpec()] * 2 + [whole()] * 7,
        out_specs=(whole(),) * 6,
        scratch_shapes=[pltpu.VMEM((LB, LB), f32)] * 3
        + [pltpu.VMEM((RB, RB), f32)] * 3
        + [pltpu.VMEM((LB, RB), f32)] * 2,
        compiler_params=pltpu.CompilerParams(vmem_limit_bytes=24 * 2**20),
        cost_estimate=pl.CostEstimate(
            flops=25_000_000_000, bytes_accessed=4_000_000, transcendentals=0
        ),
        name="refresh",
    )(spot, left_raw, gl, bl, right_raw, gr, br, tile, *squares, mine, other)


def held_kernel(factor_ref, raw_ref, g_ref, b_ref, g_out_ref, q_out_ref, s_ref, p_ref, qt_ref):
    factor = factor_ref[:1, :1]
    gram = beta_gram * g_ref[...] + (1.0 - beta_gram) * factor * factor * raw_ref[...]
    g_out_ref[...] = gram
    factorize([(gram, b_ref[...], s_ref, p_ref, qt_ref)])
    q_out_ref[...] = qt_ref[...].T


def refresh_held(factor, raw, gram, basis):
    f32 = jnp.float32
    return pl.pallas_call(
        held_kernel,
        out_shape=(shape_of(LB, LB), shape_of(LB, LB)),
        in_specs=[whole()] * 2 + [pl.BlockSpec()] * 2,
        out_specs=(whole(),) * 2,
        scratch_shapes=[pltpu.VMEM((LB, LB), f32)] * 3,
        compiler_params=pltpu.CompilerParams(vmem_limit_bytes=24 * 2**20),
        cost_estimate=pl.CostEstimate(
            flops=18_000_000_000, bytes_accessed=2_000_000, transcendentals=0
        ),
        name="refresh_held",
    )(factor, raw, gram, basis)


def own_sum_kernel(arrived_ref, out_ref):
    total = arrived_ref[0]
    for r in range(1, 32):
        total = total + arrived_ref[r]
    total = total * (1.0 / 32.0)
    for n in range(8):
        out_ref[n] = total


def right_part_kernel(tile_ref, out_ref):
    tile = tile_ref[...]
    squares = jnp.sum(tile * tile, keepdims=True)
    out_ref[...] = jnp.where(slots((RB, RB), 0, 1), squares, mm(tile, tile, 0, 0))


def right_sum_kernel(group_ref, parts_ref, out_ref, squares_ref):
    total = parts_ref[0]
    for r in range(1, 16):
        total = total + parts_ref[r]
    for n in range(16):
        out_ref[n] = total
    slot = slots((16, RB), 0, 16 * group_ref[0] + 1)
    squares = jnp.sum(jnp.where(slot, total, 0.0), keepdims=True)
    squares_ref[...] = jnp.broadcast_to(squares, squares_ref.shape)


def left_gram_kernel(*refs):
    total = mm(refs[0][...], refs[0][...], 1, 1)
    for n in range(1, 4):
        total = total + mm(refs[n][...], refs[n][...], 1, 1)
    refs[4][...] = total


def small(kernel, name, out_shape, flops, *operands, scalars=0):
    specs = [pl.BlockSpec(memory_space=pltpu.SMEM)] * scalars
    specs = specs + [whole()] * (len(operands) - scalars)
    return pl.pallas_call(
        kernel,
        out_shape=out_shape,
        in_specs=specs,
        out_specs=jax.tree.map(lambda _: whole(), out_shape),
        compiler_params=pltpu.CompilerParams(vmem_limit_bytes=16 * 2**20),
        cost_estimate=pl.CostEstimate(flops=flops, bytes_accessed=1_000_000, transcendentals=0),
        name=name,
    )(*operands)


PLACES = (0, -2, -1, -3)


def place_kernel(k_ref, *refs):
    parts, out_ref, rounded_ref, sems = refs[:-3], refs[-3], refs[-2], refs[-1]
    copies = []
    for n, shift in enumerate(PLACES):
        source = lax.rem(k_ref[0] + shift + 4, 4)
        at = pl.ds(pl.multiple_of(source * LB, 16), LB)
        rounded_ref[at, :] = parts[n][...].astype(jnp.bfloat16)
        copies.append(pltpu.make_async_copy(rounded_ref.at[at], out_ref.at[at], sems.at[n]))
        copies[-1].start()
    for copy in copies:
        copy.wait()


def place(k, parts):
    return pl.pallas_call(
        place_kernel,
        out_shape=jax.ShapeDtypeStruct((4 * LB, RB), jnp.bfloat16),
        in_specs=[pl.BlockSpec(memory_space=pltpu.SMEM)] + [whole()] * len(parts),
        out_specs=pl.BlockSpec(memory_space=pl.ANY),
        scratch_shapes=[
            pltpu.VMEM((4 * LB, RB), jnp.bfloat16),
            pltpu.SemaphoreType.DMA((len(PLACES),)),
        ],
        compiler_params=pltpu.CompilerParams(vmem_limit_bytes=16 * 2**20),
        name="place",
    )(k, *parts)


def gather_all(x, axes, count):
    copies = jnp.broadcast_to(x[None], (count,) + x.shape)
    return lax.all_to_all(copies, axes, 0, 0, tiled=True)


def shift_perm(size, by):
    return [(s, (s + by) % size) for s in range(size)]


def shards(
    pseudo_grads, left_gram, right_gram, left_basis, right_basis, first_moment, second_moment
):
    k = lax.axis_index("yk")
    x = lax.axis_index("x")

    ours = jnp.concatenate([first_moment, second_moment], axis=0)
    column = [ours] + [lax.ppermute(ours, "zh", shift_perm(4, by)) for by in range(1, 4)]

    held = jnp.concatenate([left_gram, left_basis], axis=0)
    moved = jnp.where(x == k, held, 0.0)
    for by in range(1, 4):
        moved = moved + lax.ppermute(
            held, ("yk", "x"), [(b * 4 + b, b * 4 + (b + by) % 4) for b in range(4)]
        )

    pieces = pseudo_grads[0].astype(jnp.float32).reshape(32, 40, RB)
    arrived = lax.all_to_all(pieces, REP, 0, 0, tiled=True)
    arrived, moved = lax.optimization_barrier((arrived, moved))
    copies = small(own_sum_kernel, "own_sum", shape_of(8, 40, RB), 10**8, arrived)
    copies, *column = lax.optimization_barrier((copies, *column))
    tile = lax.all_to_all(copies, MEMBERS, 0, 0, tiled=True).reshape(LB, RB)
    mine = jnp.concatenate(column, axis=0)
    other = lax.ppermute(mine, "y2", shift_perm(2, 1))
    tile, mine, other = lax.optimization_barrier((tile, mine, other))

    right_part = small(right_part_kernel, "right_part", shape_of(RB, RB), 10**9, tile)
    sent, right_part = lax.optimization_barrier((tile, right_part))
    parts = lax.all_to_all(right_part.reshape(16, 16, RB), RIGHT_GROUP, 0, 0, tiled=True)
    tiles = [tile] + [lax.ppermute(sent, "x", shift_perm(4, by)) for by in range(1, 4)]
    right_own, squares_own = small(
        right_sum_kernel, "right_sum", (shape_of(16, 16, RB), shape_of(8, 128)), 10**8,
        lax.axis_index(RIGHT_GROUP).astype(jnp.int32).reshape(1), parts, scalars=1,
    )
    right_raw = lax.all_to_all(right_own, RIGHT_GROUP, 0, 0, tiled=True).reshape(RB, RB)
    squares = [squares_own] + [
        lax.ppermute(squares_own, "x", shift_perm(4, by)) for by in range(1, 4)
    ]
    left_raw = small(left_gram_kernel, "left_gram", shape_of(LB, LB), 2 * 10**9, *tiles)
    swap = [(a * 4 + b, b * 4 + a) for a in range(4) for b in range(4)]
    held_raw = lax.ppermute(left_raw, ("yk", "x"), swap)

    right_new, right_basis_new, moment, second, turned, factor = refresh(
        jnp.stack([lax.axis_index("y2"), lax.axis_index("zh")]).astype(jnp.int32), left_raw,
        moved[0], moved[1], right_raw, right_gram[0], right_basis[0], tile, squares, mine, other,
    )

    blocks = [turned] + [lax.ppermute(turned, "yk", shift_perm(4, by)) for by in (2, 1, 3)]
    left_new, left_basis_new = refresh_held(factor, held_raw, left_gram[0], left_basis[0])
    *blocks, left_new, left_basis_new = lax.optimization_barrier(
        (*blocks, left_new, left_basis_new)
    )
    update = place(k.astype(jnp.int32).reshape(1), blocks)
    return (
        update, left_new[None], left_basis_new[None], right_new[None], right_basis_new[None],
        moment, second,
    )


def solution(mesh):
    fine = Mesh(
        mesh.devices.reshape(4, 2, 4, 2, 2, 4), ("yk", "y2", "zh", "zl", "core", "x")
    )
    left = P(ROW + ("x",), None, None)
    right = P("x", None, None)
    moments = P(ROW + REP, "x")
    return jax.shard_map(
        shards,
        mesh=fine,
        in_specs=(P(REP, ROW, "x"), left, right, left, right, moments, moments),
        out_specs=(P(ROW, "x"), left, left, right, right, moments, moments),
        check_vma=False,
    )
```

```python
import math

import jax
import jax.numpy as jnp
from jax import lax
from jax.experimental import pallas as pl
from jax.experimental.pallas import tpu as pltpu
from jax.sharding import Mesh, PartitionSpec as P

D = 5120
KV = 1024
LB = 320
RB = 256
NB = 64

highest = lax.Precision.HIGHEST
beta_gram = 0.95
beta_first = 0.95
beta_second = 0.95
first_bias = 1.0 - 0.95**4
second_bias = 1.0 - 0.95**4
clip_ratio = 0.5

REP = ("yk", "y2", "zh")
ROW = ("zl", "core")
MEMBERS = ("y2", "zh")
RIGHT_GROUP = ("yk", "zl", "core")


def mm(a, b, ca=1, cb=0):
    return lax.dot_general(
        a, b, (((ca,), (cb,)), ((), ())), precision=highest, preferred_element_type=jnp.float32
    )


def eliminate(rows, off):
    row_id = lax.broadcasted_iota(jnp.int32, (8, 128), 0)
    for g in range(8):
        count = 8 - g
        cols = [
            [
                jnp.broadcast_to(rows[g + h][:, off + 8 * g + t : off + 8 * g + t + 1], (8, 128))
                for h in range(count)
            ]
            for t in range(8)
        ]
        pivots = jnp.ones((8, 128), jnp.float32)
        for t in range(8):
            pivot = jnp.broadcast_to(cols[t][0][t : t + 1, :], (8, 128))
            inv = 1.0 / pivot
            pivots = jnp.where(row_id == t, pivot, pivots)
            f = [c * inv for c in cols[t]]
            f[0] = jnp.where(row_id > t, f[0], 0.0)
            for u in range(t + 1, 8):
                lead = jnp.broadcast_to(cols[u][0][t : t + 1, :], (8, 128))
                cols[u] = [c - fh * lead for c, fh in zip(cols[u], f)]
            lead = jnp.broadcast_to(rows[g][t : t + 1, :], (8, 128))
            for h in range(count):
                rows[g + h] = rows[g + h] - f[h] * lead
            yield
        scale = lax.rsqrt(pivots)
        scale = scale * (1.5 - 0.5 * pivots * scale * scale)
        rows[g] = rows[g] * scale


def load_block(s_ref, at):
    base = (at // 128) * 128
    off = at - base
    other = 64 - off
    width = min(128, s_ref.shape[1] - base)
    lane = lax.broadcasted_iota(jnp.int32, (8, 128), 1)
    row = lax.broadcasted_iota(jnp.int32, (8, 128), 0)
    rows = []
    for g in range(8):
        piece = s_ref[at + 8 * g : at + 8 * g + 8, base : base + width]
        if width < 128:
            piece = jnp.concatenate([piece, jnp.zeros((8, 128 - width), jnp.float32)], axis=1)
        eye = (lane == row + (8 * g + other)).astype(jnp.float32)
        rows.append(jnp.where((lane >= off) & (lane < off + 64), piece, eye))
    return rows, off, other


def apply_block(rows, other, s_ref, pt_ref, qt_ref, at):
    n = s_ref.shape[0]
    inv = jnp.concatenate(rows, axis=0)
    if other:
        inv = pltpu.roll(inv, 64, axis=1)
    inv = inv[:, :64]
    wp = mm(inv, pt_ref[at : at + 64, :])
    qt_ref[at : at + 64, :] = wp
    if at + 64 < n:
        start = ((at + 64) // 128) * 128
        ws = mm(inv, s_ref[at : at + 64, start:])
        s_ref[start:, start:] = s_ref[start:, start:] - mm(ws, ws, 0, 0)
        pt_ref[start:, :] = pt_ref[start:, :] - mm(ws, wp, 0, 0)


def factorize(jobs):
    for gram, basis, s_ref, p_ref, _ in jobs:
        pt = mm(basis, gram, 0, 0)
        p_ref[...] = pt
        s_ref[...] = mm(pt, pt, 1, 1)
    for step in range(LB // NB):
        at = step * NB
        blocks = []
        for _, _, s_ref, p_ref, qt_ref in jobs:
            if at < s_ref.shape[0]:
                rows, off, other = load_block(s_ref, at)
                blocks.append((rows, other, s_ref, p_ref, qt_ref, eliminate(rows, off)))
        live = [b[5] for b in blocks]
        while live:
            live = [g for g in live if next(g, 1) is None]
        for rows, other, s_ref, p_ref, qt_ref, _ in blocks:
            apply_block(rows, other, s_ref, p_ref, qt_ref, at)


def slots(shape, row_at, col_at):
    row = lax.broadcasted_iota(jnp.int32, shape, 0)
    col = lax.broadcasted_iota(jnp.int32, shape, 1)
    return (row % 16 == row_at) & (col == row + col_at)


def refresh_kernel(
    member_ref, left_raw_ref, moved_ref, right_raw_ref, gr_ref, br_ref, tile_ref, sq0_ref, sq1_ref,
    sq2_ref, sq3_ref, mine_ref, other_ref,
    gr_out_ref, qr_out_ref, m_ref, v_ref, u_ref, factor_ref,
    sl_ref, pl_ref, qlt_ref, sr_ref, pr_ref, qrt_ref, ms_ref, vs_ref,
):
    y2, zh = member_ref[0] // 4, lax.rem(member_ref[0], 4)
    for src_ref, pair in ((mine_ref, y2), (other_ref, 1 - y2)):
        for n, shift in enumerate((0, -1, -2, -3)):
            at = pl.multiple_of(40 * (4 * pair + lax.rem(zh + shift + 4, 4)), 8)
            ms_ref[pl.ds(at, 40), :] = src_ref[80 * n : 80 * n + 40, :]
            vs_ref[pl.ds(at, 40), :] = src_ref[80 * n + 40 : 80 * n + 80, :]
    packed = right_raw_ref[...]
    slot = slots((RB, RB), 0, 1)
    right_raw = jnp.where(slot, packed.T, packed)
    total = (sq0_ref[...] + sq1_ref[...] + (sq2_ref[...] + sq3_ref[...]))[:1, :1]
    factor = clip_ratio * math.sqrt(D * KV) / (jnp.sqrt(total) + 1e-06)
    factor_ref[...] = jnp.broadcast_to(factor, factor_ref.shape)
    weight = (1.0 - beta_gram) * factor * factor
    right_new = beta_gram * gr_ref[...] + weight * right_raw
    gr_out_ref[...] = right_new
    left_new = beta_gram * moved_ref[0] + weight * left_raw_ref[...]
    factorize(
        [
            (left_new, moved_ref[1], sl_ref, pl_ref, qlt_ref),
            (right_new, br_ref[...], sr_ref, pr_ref, qrt_ref),
        ]
    )
    qrt = qrt_ref[...]
    qr_out_ref[...] = qrt.T
    rotated = mm(mm(qlt_ref[...], tile_ref[...]) * factor, qrt, 1, 1)
    moment = beta_first * ms_ref[...] + (1.0 - beta_first) * rotated
    second = beta_second * vs_ref[...] + (1.0 - beta_second) * rotated * rotated
    ms_ref[...] = moment
    vs_ref[...] = second
    direction = moment / first_bias / (jnp.sqrt(second / second_bias) + 1e-08)
    u_ref[...] = mm(qlt_ref[...], mm(direction, qrt), 0, 0)
    own = pl.ds(pl.multiple_of(40 * (4 * y2 + zh), 8), 40)
    m_ref[...] = ms_ref[own, :]
    v_ref[...] = vs_ref[own, :]


def shape_of(*dims):
    return jax.ShapeDtypeStruct(dims, jnp.float32)


def whole():
    return pl.BlockSpec(memory_space=pltpu.VMEM)


def refresh(member, left_raw, moved, right_raw, gr, br, tile, squares, mine, other):
    f32 = jnp.float32
    return pl.pallas_call(
        refresh_kernel,
        out_shape=(
            shape_of(RB, RB), shape_of(RB, RB), shape_of(40, RB), shape_of(40, RB),
            shape_of(LB, RB), shape_of(8, 128),
        ),
        in_specs=[pl.BlockSpec(memory_space=pltpu.SMEM)] + [whole()] * 12,
        out_specs=(whole(),) * 6,
        scratch_shapes=[pltpu.VMEM((LB, LB), f32)] * 3
        + [pltpu.VMEM((RB, RB), f32)] * 3
        + [pltpu.VMEM((LB, RB), f32)] * 2,
        compiler_params=pltpu.CompilerParams(vmem_limit_bytes=12 * 2**20),
        cost_estimate=pl.CostEstimate(
            flops=25_000_000_000, bytes_accessed=4_000_000, transcendentals=0
        ),
        name="refresh",
    )(member, left_raw, moved, right_raw, gr, br, tile, *squares, mine, other)


def held_kernel(factor_ref, raw_ref, g_ref, b_ref, g_out_ref, q_out_ref, s_ref, p_ref, qt_ref):
    factor = factor_ref[:1, :1]
    gram = beta_gram * g_ref[...] + (1.0 - beta_gram) * factor * factor * raw_ref[...]
    g_out_ref[...] = gram
    factorize([(gram, b_ref[...], s_ref, p_ref, qt_ref)])
    q_out_ref[...] = qt_ref[...].T


def refresh_held(factor, raw, gram, basis):
    f32 = jnp.float32
    return pl.pallas_call(
        held_kernel,
        out_shape=(shape_of(LB, LB), shape_of(LB, LB)),
        in_specs=[whole()] * 4,
        out_specs=(whole(),) * 2,
        scratch_shapes=[pltpu.VMEM((LB, LB), f32)] * 3,
        compiler_params=pltpu.CompilerParams(vmem_limit_bytes=12 * 2**20),
        cost_estimate=pl.CostEstimate(
            flops=18_000_000_000, bytes_accessed=2_000_000, transcendentals=0
        ),
        name="refresh_held",
    )(factor, raw, gram, basis)


def own_sum_kernel(arrived_ref, out_ref):
    total = arrived_ref[0]
    for r in range(1, 32):
        total = total + arrived_ref[r]
    total = total * (1.0 / 32.0)
    for n in range(8):
        out_ref[n] = total


def right_part_kernel(tile_ref, out_ref):
    tile = tile_ref[...]
    squares = jnp.sum(tile * tile, keepdims=True)
    out_ref[...] = jnp.where(slots((RB, RB), 0, 1), squares, mm(tile, tile, 0, 0))


def right_sum_kernel(group_ref, parts_ref, out_ref, squares_ref):
    total = parts_ref[0]
    for r in range(1, 16):
        total = total + parts_ref[r]
    for n in range(16):
        out_ref[n] = total
    slot = slots((16, RB), 0, 16 * group_ref[0] + 1)
    squares = jnp.sum(jnp.where(slot, total, 0.0), keepdims=True)
    squares_ref[...] = jnp.broadcast_to(squares, squares_ref.shape)


def left_gram_kernel(*refs):
    total = mm(refs[0][...], refs[0][...], 1, 1)
    for n in range(1, 4):
        total = total + mm(refs[n][...], refs[n][...], 1, 1)
    refs[4][...] = total


def small(kernel, name, out_shape, flops, *operands, scalars=0):
    specs = [pl.BlockSpec(memory_space=pltpu.SMEM)] * scalars
    specs = specs + [whole()] * (len(operands) - scalars)
    return pl.pallas_call(
        kernel,
        out_shape=out_shape,
        in_specs=specs,
        out_specs=jax.tree.map(lambda _: whole(), out_shape),
        compiler_params=pltpu.CompilerParams(vmem_limit_bytes=6 * 2**20),
        cost_estimate=pl.CostEstimate(flops=flops, bytes_accessed=1_000_000, transcendentals=0),
        name=name,
    )(*operands)


def place_kernel(blocks_ref, out_ref, rounded_ref, sems):
    copies = []
    for n in range(4):
        rounded_ref[n * LB : (n + 1) * LB, :] = blocks_ref[n].astype(jnp.bfloat16)
        at = pl.ds(n * LB, LB)
        copies.append(pltpu.make_async_copy(rounded_ref.at[at], out_ref.at[at], sems.at[n]))
        copies[-1].start()
    for copy in copies:
        copy.wait()


def place(blocks):
    return pl.pallas_call(
        place_kernel,
        out_shape=jax.ShapeDtypeStruct((4 * LB, RB), jnp.bfloat16),
        in_specs=[whole()],
        out_specs=pl.BlockSpec(memory_space=pl.ANY),
        scratch_shapes=[
            pltpu.VMEM((4 * LB, RB), jnp.bfloat16),
            pltpu.SemaphoreType.DMA((4,)),
        ],
        compiler_params=pltpu.CompilerParams(vmem_limit_bytes=6 * 2**20),
        name="place",
    )(blocks)


def gather_all(x, axes, count):
    copies = jnp.broadcast_to(x[None], (count,) + x.shape)
    return lax.all_to_all(copies, axes, 0, 0, tiled=True)


def shift_perm(size, by):
    return [(s, (s + by) % size) for s in range(size)]


def shards(
    pseudo_grads, left_gram, right_gram, left_basis, right_basis, first_moment, second_moment
):
    k = lax.axis_index("yk")
    x = lax.axis_index("x")

    ours = jnp.concatenate([first_moment, second_moment], axis=0)
    column = [ours] + [lax.ppermute(ours, "zh", shift_perm(4, by)) for by in range(1, 4)]

    held = jnp.concatenate([left_gram, left_basis], axis=0)
    moved = jnp.where(x == k, held, 0.0)
    for by in range(1, 4):
        moved = moved + lax.ppermute(
            held, ("yk", "x"), [(b * 4 + b, b * 4 + (b + by) % 4) for b in range(4)]
        )

    pieces = pseudo_grads[0].astype(jnp.float32).reshape(32, 40, RB)
    arrived = lax.all_to_all(pieces, REP, 0, 0, tiled=True)
    copies = small(own_sum_kernel, "own_sum", shape_of(8, 40, RB), 10**8, arrived)
    copies, *column = lax.optimization_barrier((copies, *column))
    tile = lax.all_to_all(copies, MEMBERS, 0, 0, tiled=True).reshape(LB, RB)
    mine = jnp.concatenate(column, axis=0)
    other = lax.ppermute(mine, "y2", shift_perm(2, 1))
    tile, mine, other, moved = lax.optimization_barrier((tile, mine, other, moved))

    right_part = small(right_part_kernel, "right_part", shape_of(RB, RB), 10**9, tile)
    sent, right_part = lax.optimization_barrier((tile, right_part))
    parts = lax.all_to_all(right_part.reshape(16, 16, RB), RIGHT_GROUP, 0, 0, tiled=True)
    tiles = [tile] + [lax.ppermute(sent, "x", shift_perm(4, by)) for by in range(1, 4)]
    right_own, squares_own = small(
        right_sum_kernel, "right_sum", (shape_of(16, 16, RB), shape_of(8, 128)), 10**8,
        lax.axis_index(RIGHT_GROUP).astype(jnp.int32).reshape(1), parts, scalars=1,
    )
    right_raw = lax.all_to_all(right_own, RIGHT_GROUP, 0, 0, tiled=True).reshape(RB, RB)
    squares = [squares_own] + [
        lax.ppermute(squares_own, "x", shift_perm(4, by)) for by in range(1, 4)
    ]
    left_raw = small(left_gram_kernel, "left_gram", shape_of(LB, LB), 2 * 10**9, *tiles)
    along_y = [(j * 4 + c, (c - j) % 4 * 4 + c) for j in range(4) for c in range(4)]
    along_x = [(g * 4 + c, g * 4 + (c - g) % 4) for g in range(4) for c in range(4)]
    passed = lax.ppermute(left_raw, ("yk", "x"), along_y)

    right_new, right_basis_new, moment, second, turned, factor = refresh(
        lax.axis_index(MEMBERS).astype(jnp.int32).reshape(1), left_raw, moved, right_raw,
        right_gram[0], right_basis[0], tile, squares, mine, other,
    )

    held_raw = lax.ppermute(passed, ("yk", "x"), along_x)
    blocks = gather_all(turned, "yk", 4)
    left_new, left_basis_new = refresh_held(factor, held_raw, left_gram[0], left_basis[0])
    blocks, left_new, left_basis_new = lax.optimization_barrier(
        (blocks, left_new, left_basis_new)
    )
    update = place(blocks)
    return (
        update, left_new[None], left_basis_new[None], right_new[None], right_basis_new[None],
        moment, second,
    )


def solution(mesh):
    fine = Mesh(
        mesh.devices.reshape(4, 2, 4, 2, 2, 4), ("yk", "y2", "zh", "zl", "core", "x")
    )
    left = P(ROW + ("x",), None, None)
    right = P("x", None, None)
    moments = P(ROW + REP, "x")
    return jax.shard_map(
        shards,
        mesh=fine,
        in_specs=(P(REP, ROW, "x"), left, right, left, right, moments, moments),
        out_specs=(P(ROW, "x"), left, left, right, right, moments, moments),
        check_vma=False,
    )
```

```python
import math

import jax
import jax.numpy as jnp
from jax import lax
from jax.experimental import pallas as pl
from jax.experimental.pallas import tpu as pltpu
from jax.sharding import Mesh, PartitionSpec as P

D = 5120
KV = 1024
LB = 320
RB = 256
NB = 64

highest = lax.Precision.HIGHEST
beta_gram = 0.95
beta_first = 0.95
beta_second = 0.95
first_bias = 1.0 - 0.95**4
second_bias = 1.0 - 0.95**4
clip_ratio = 0.5

REP = ("yk", "y2", "zh")
ROW = ("zl", "core")
MEMBERS = ("y2", "zh")
RIGHT_GROUP = ("yk", "zl", "core")


def mm(a, b, ca=1, cb=0):
    return lax.dot_general(
        a, b, (((ca,), (cb,)), ((), ())), precision=highest, preferred_element_type=jnp.float32
    )


def eliminate(rows, off):
    row_id = lax.broadcasted_iota(jnp.int32, (8, 128), 0)
    for g in range(8):
        count = 8 - g
        cols = [
            [
                jnp.broadcast_to(rows[g + h][:, off + 8 * g + t : off + 8 * g + t + 1], (8, 128))
                for h in range(count)
            ]
            for t in range(8)
        ]
        pivots = jnp.ones((8, 128), jnp.float32)
        for t in range(8):
            pivot = jnp.broadcast_to(cols[t][0][t : t + 1, :], (8, 128))
            inv = 1.0 / pivot
            pivots = jnp.where(row_id == t, pivot, pivots)
            f = [c * inv for c in cols[t]]
            f[0] = jnp.where(row_id > t, f[0], 0.0)
            for u in range(t + 1, 8):
                lead = jnp.broadcast_to(cols[u][0][t : t + 1, :], (8, 128))
                cols[u] = [c - fh * lead for c, fh in zip(cols[u], f)]
            lead = jnp.broadcast_to(rows[g][t : t + 1, :], (8, 128))
            for h in range(count):
                rows[g + h] = rows[g + h] - f[h] * lead
            yield
        scale = lax.rsqrt(pivots)
        scale = scale * (1.5 - 0.5 * pivots * scale * scale)
        rows[g] = rows[g] * scale


def load_block(s_ref, at):
    base = (at // 128) * 128
    off = at - base
    other = 64 - off
    width = min(128, s_ref.shape[1] - base)
    lane = lax.broadcasted_iota(jnp.int32, (8, 128), 1)
    row = lax.broadcasted_iota(jnp.int32, (8, 128), 0)
    rows = []
    for g in range(8):
        piece = s_ref[at + 8 * g : at + 8 * g + 8, base : base + width]
        if width < 128:
            piece = jnp.concatenate([piece, jnp.zeros((8, 128 - width), jnp.float32)], axis=1)
        eye = (lane == row + (8 * g + other)).astype(jnp.float32)
        rows.append(jnp.where((lane >= off) & (lane < off + 64), piece, eye))
    return rows, off, other


def apply_block(rows, other, s_ref, pt_ref, qt_ref, at):
    n = s_ref.shape[0]
    inv = jnp.concatenate(rows, axis=0)
    if other:
        inv = pltpu.roll(inv, 64, axis=1)
    inv = inv[:, :64]
    wp = mm(inv, pt_ref[at : at + 64, :])
    qt_ref[at : at + 64, :] = wp
    if at + 64 < n:
        start = ((at + 64) // 128) * 128
        ws = mm(inv, s_ref[at : at + 64, start:])
        s_ref[start:, start:] = s_ref[start:, start:] - mm(ws, ws, 0, 0)
        pt_ref[start:, :] = pt_ref[start:, :] - mm(ws, wp, 0, 0)


def factorize(jobs):
    for gram, basis, s_ref, p_ref, _ in jobs:
        pt = mm(basis, gram, 0, 0)
        p_ref[...] = pt
        s_ref[...] = mm(pt, pt, 1, 1)
    for step in range(LB // NB):
        at = step * NB
        blocks = []
        for _, _, s_ref, p_ref, qt_ref in jobs:
            if at < s_ref.shape[0]:
                rows, off, other = load_block(s_ref, at)
                blocks.append((rows, other, s_ref, p_ref, qt_ref, eliminate(rows, off)))
        live = [b[5] for b in blocks]
        while live:
            live = [g for g in live if next(g, 1) is None]
        for rows, other, s_ref, p_ref, qt_ref, _ in blocks:
            apply_block(rows, other, s_ref, p_ref, qt_ref, at)


def slots(shape, row_at, col_at):
    row = lax.broadcasted_iota(jnp.int32, shape, 0)
    col = lax.broadcasted_iota(jnp.int32, shape, 1)
    return (row % 16 == row_at) & (col == row + col_at)


def refresh_kernel(
    member_ref, left_raw_ref, moved_ref, right_raw_ref, tile_ref, gr_hbm, br_hbm, mine_hbm, other_hbm,
    gr_out_ref, qr_out_ref, m_ref, v_ref, u_ref, factor_ref,
    sl_ref, pl_ref, qlt_ref, sr_ref, pr_ref, qrt_ref, ms_ref, vs_ref,
    gr_ref, br_ref, mine_ref, other_ref, sems,
):
    fetched = [
        pltpu.make_async_copy(src, dst, sems.at[n])
        for n, (src, dst) in enumerate(
            ((gr_hbm, gr_ref), (br_hbm, br_ref), (mine_hbm, mine_ref), (other_hbm, other_ref))
        )
    ]
    for copy in fetched:
        copy.start()
    y2, zh = member_ref[0] // 4, lax.rem(member_ref[0], 4)
    packed = right_raw_ref[...]
    slot = slots((RB, RB), 0, 1)
    right_raw = jnp.where(slot, packed.T, packed)
    total = jnp.sum(jnp.where(slot, packed, 0.0), keepdims=True)
    factor = clip_ratio * math.sqrt(D * KV) / (jnp.sqrt(total) + 1e-06)
    factor_ref[...] = jnp.broadcast_to(factor, factor_ref.shape)
    weight = (1.0 - beta_gram) * factor * factor
    fetched[0].wait()
    fetched[1].wait()
    right_new = beta_gram * gr_ref[...] + weight * right_raw
    gr_out_ref[...] = right_new
    left_new = beta_gram * moved_ref[0] + weight * left_raw_ref[...]
    factorize(
        [
            (left_new, moved_ref[1], sl_ref, pl_ref, qlt_ref),
            (right_new, br_ref[...], sr_ref, pr_ref, qrt_ref),
        ]
    )
    qrt = qrt_ref[...]
    qr_out_ref[...] = qrt.T
    rotated = mm(mm(qlt_ref[...], tile_ref[...]) * factor, qrt, 1, 1)
    fetched[2].wait()
    fetched[3].wait()
    for src_ref, pair in ((mine_ref, y2), (other_ref, 1 - y2)):
        for n, shift in enumerate((0, -1, -2, -3)):
            at = pl.multiple_of(40 * (4 * pair + lax.rem(zh + shift + 4, 4)), 8)
            ms_ref[pl.ds(at, 40), :] = src_ref[80 * n : 80 * n + 40, :]
            vs_ref[pl.ds(at, 40), :] = src_ref[80 * n + 40 : 80 * n + 80, :]
    moment = beta_first * ms_ref[...] + (1.0 - beta_first) * rotated
    second = beta_second * vs_ref[...] + (1.0 - beta_second) * rotated * rotated
    ms_ref[...] = moment
    vs_ref[...] = second
    direction = moment / first_bias / (jnp.sqrt(second / second_bias) + 1e-08)
    u_ref[...] = mm(qlt_ref[...], mm(direction, qrt), 0, 0)
    own = pl.ds(pl.multiple_of(40 * (4 * y2 + zh), 8), 40)
    m_ref[...] = ms_ref[own, :]
    v_ref[...] = vs_ref[own, :]


def shape_of(*dims):
    return jax.ShapeDtypeStruct(dims, jnp.float32)


def whole():
    return pl.BlockSpec(memory_space=pltpu.VMEM)


def refresh(member, left_raw, moved, right_raw, tile, gr, br, mine, other):
    f32 = jnp.float32
    return pl.pallas_call(
        refresh_kernel,
        out_shape=(
            shape_of(RB, RB), shape_of(RB, RB), shape_of(40, RB), shape_of(40, RB),
            shape_of(LB, RB), shape_of(8, 128),
        ),
        in_specs=[pl.BlockSpec(memory_space=pltpu.SMEM)]
        + [whole()] * 4
        + [pl.BlockSpec(memory_space=pl.ANY)] * 4,
        out_specs=(whole(),) * 6,
        scratch_shapes=[pltpu.VMEM((LB, LB), f32)] * 3
        + [pltpu.VMEM((RB, RB), f32)] * 3
        + [pltpu.VMEM((LB, RB), f32)] * 2
        + [pltpu.VMEM((RB, RB), f32)] * 2
        + [pltpu.VMEM((LB, RB), f32)] * 2
        + [pltpu.SemaphoreType.DMA((4,))],
        compiler_params=pltpu.CompilerParams(vmem_limit_bytes=12 * 2**20),
        cost_estimate=pl.CostEstimate(
            flops=25_000_000_000, bytes_accessed=4_000_000, transcendentals=0
        ),
        name="refresh",
    )(member, left_raw, moved, right_raw, tile, gr, br, mine, other)


def held_kernel(factor_ref, raw_ref, g_ref, b_ref, g_out_ref, q_out_ref, s_ref, p_ref, qt_ref):
    factor = factor_ref[:1, :1]
    gram = beta_gram * g_ref[...] + (1.0 - beta_gram) * factor * factor * raw_ref[...]
    g_out_ref[...] = gram
    factorize([(gram, b_ref[...], s_ref, p_ref, qt_ref)])
    q_out_ref[...] = qt_ref[...].T


def refresh_held(factor, raw, gram, basis):
    f32 = jnp.float32
    return pl.pallas_call(
        held_kernel,
        out_shape=(shape_of(LB, LB), shape_of(LB, LB)),
        in_specs=[whole()] * 4,
        out_specs=(whole(),) * 2,
        scratch_shapes=[pltpu.VMEM((LB, LB), f32)] * 3,
        compiler_params=pltpu.CompilerParams(vmem_limit_bytes=12 * 2**20),
        cost_estimate=pl.CostEstimate(
            flops=18_000_000_000, bytes_accessed=2_000_000, transcendentals=0
        ),
        name="refresh_held",
    )(factor, raw, gram, basis)


def own_sum_kernel(arrived_ref, out_ref):
    total = arrived_ref[0]
    for r in range(1, 32):
        total = total + arrived_ref[r]
    total = total * (1.0 / 32.0)
    for n in range(8):
        out_ref[n] = total


def right_part_kernel(tile_ref, out_ref):
    tile = tile_ref[...]
    out_ref[...] = mm(tile, tile, 0, 0)


def fetch(refs, landed_ref, sems):
    copies = [
        pltpu.make_async_copy(ref, landed_ref.at[n], sems.at[n]) for n, ref in enumerate(refs)
    ]
    for copy in copies:
        copy.start()
    return copies


def right_sum_kernel(group_ref, parts_ref, tile_ref, *refs):
    others, out_ref, landed_ref, sems = refs[:3], refs[3], refs[4], refs[5]
    copies = fetch(others, landed_ref, sems)
    total = parts_ref[0]
    for r in range(1, 16):
        total = total + parts_ref[r]
    squares = jnp.sum(tile_ref[...] * tile_ref[...], keepdims=True)
    for n, copy in enumerate(copies):
        copy.wait()
        squares = squares + jnp.sum(landed_ref[n] * landed_ref[n], keepdims=True)
    total = jnp.where(slots((16, RB), 0, 16 * group_ref[0] + 1), squares, total)
    for n in range(16):
        out_ref[n] = total


def left_gram_kernel(tile_ref, *refs):
    others, out_ref, landed_ref, sems = refs[:3], refs[3], refs[4], refs[5]
    copies = fetch(others, landed_ref, sems)
    total = mm(tile_ref[...], tile_ref[...], 1, 1)
    for n, copy in enumerate(copies):
        copy.wait()
        total = total + mm(landed_ref[n], landed_ref[n], 1, 1)
    out_ref[...] = total


def small(kernel, name, out_shape, flops, *operands, scalars=0, places=0):
    specs = [pl.BlockSpec(memory_space=pltpu.SMEM)] * scalars
    specs = specs + [whole()] * (len(operands) - scalars - places)
    specs = specs + [pl.BlockSpec(memory_space=pl.ANY)] * places
    scratch = [pltpu.VMEM((places, LB, RB), jnp.float32), pltpu.SemaphoreType.DMA((places,))]
    return pl.pallas_call(
        kernel,
        out_shape=out_shape,
        in_specs=specs,
        out_specs=whole(),
        scratch_shapes=scratch if places else [],
        compiler_params=pltpu.CompilerParams(vmem_limit_bytes=6 * 2**20),
        cost_estimate=pl.CostEstimate(flops=flops, bytes_accessed=1_000_000, transcendentals=0),
        name=name,
    )(*operands)


def place_kernel(blocks_ref, out_ref, rounded_ref, sems):
    copies = []
    for n in range(4):
        rounded_ref[n * LB : (n + 1) * LB, :] = blocks_ref[n].astype(jnp.bfloat16)
        at = pl.ds(n * LB, LB)
        copies.append(pltpu.make_async_copy(rounded_ref.at[at], out_ref.at[at], sems.at[n]))
        copies[-1].start()
    for copy in copies:
        copy.wait()


def place(blocks):
    return pl.pallas_call(
        place_kernel,
        out_shape=jax.ShapeDtypeStruct((4 * LB, RB), jnp.bfloat16),
        in_specs=[whole()],
        out_specs=pl.BlockSpec(memory_space=pl.ANY),
        scratch_shapes=[
            pltpu.VMEM((4 * LB, RB), jnp.bfloat16),
            pltpu.SemaphoreType.DMA((4,)),
        ],
        compiler_params=pltpu.CompilerParams(vmem_limit_bytes=6 * 2**20),
        name="place",
    )(blocks)


def gather_all(x, axes, count):
    copies = jnp.broadcast_to(x[None], (count,) + x.shape)
    return lax.all_to_all(copies, axes, 0, 0, tiled=True)


def shift_perm(size, by):
    return [(s, (s + by) % size) for s in range(size)]


def shards(
    pseudo_grads, left_gram, right_gram, left_basis, right_basis, first_moment, second_moment
):
    k = lax.axis_index("yk")
    x = lax.axis_index("x")

    ours = jnp.concatenate([first_moment, second_moment], axis=0)
    column = [ours] + [lax.ppermute(ours, "zh", shift_perm(4, by)) for by in range(1, 4)]

    held = jnp.concatenate([left_gram, left_basis], axis=0)
    near = lax.ppermute(held, ("yk", "x"), [(b * 4 + b, b * 4 + (b + 1) % 4) for b in range(4)])
    near = jnp.where(x == k, held, near)
    far = lax.ppermute(
        near, ("yk", "x"),
        [(b * 4 + (b + n) % 4, b * 4 + (b + n + 2) % 4) for b in range(4) for n in range(2)],
    )
    moved = near + far

    pieces = pseudo_grads[0].astype(jnp.float32).reshape(32, 40, RB)
    arrived = lax.all_to_all(pieces, REP, 0, 0, tiled=True)
    copies = small(own_sum_kernel, "own_sum", shape_of(8, 40, RB), 10**8, arrived)
    _, *column = lax.optimization_barrier((copies, *column))
    tile = lax.all_to_all(copies, MEMBERS, 0, 0, tiled=True).reshape(LB, RB)
    mine = jnp.concatenate(column, axis=0)
    other = lax.ppermute(mine, "y2", shift_perm(2, 1))
    tile, mine, other, moved = lax.optimization_barrier((tile, mine, other, moved))

    right_part = small(right_part_kernel, "right_part", shape_of(RB, RB), 10**9, tile)
    sent, right_part = lax.optimization_barrier((tile, right_part))
    parts = lax.all_to_all(right_part.reshape(16, 16, RB), RIGHT_GROUP, 0, 0, tiled=True)
    tiles = [lax.ppermute(sent, "x", shift_perm(4, by)) for by in range(1, 4)]
    right_own = small(
        right_sum_kernel, "right_sum", shape_of(16, 16, RB), 10**8,
        lax.axis_index(RIGHT_GROUP).astype(jnp.int32).reshape(1), parts, tile, *tiles,
        scalars=1, places=3,
    )
    right_raw = lax.all_to_all(right_own, RIGHT_GROUP, 0, 0, tiled=True).reshape(RB, RB)
    left_raw = small(left_gram_kernel, "left_gram", shape_of(LB, LB), 2 * 10**9, tile, *tiles, places=3)
    along_y = [(j * 4 + c, (c - j) % 4 * 4 + c) for j in range(4) for c in range(4)]
    along_x = [(g * 4 + c, g * 4 + (c - g) % 4) for g in range(4) for c in range(4)]
    passed = lax.ppermute(left_raw, ("yk", "x"), along_y)

    right_new, right_basis_new, moment, second, turned, factor = refresh(
        lax.axis_index(MEMBERS).astype(jnp.int32).reshape(1), left_raw, moved, right_raw,
        tile, right_gram[0], right_basis[0], mine, other,
    )

    passed, turned = lax.optimization_barrier((passed, turned))
    held_raw = lax.ppermute(passed, ("yk", "x"), along_x)
    blocks = gather_all(turned, "yk", 4)
    left_new, left_basis_new = refresh_held(factor, held_raw, left_gram[0], left_basis[0])
    blocks, left_new, left_basis_new = lax.optimization_barrier(
        (blocks, left_new, left_basis_new)
    )
    update = place(blocks)
    return (
        update, left_new[None], left_basis_new[None], right_new[None], right_basis_new[None],
        moment, second,
    )


def solution(mesh):
    fine = Mesh(
        mesh.devices.reshape(4, 2, 4, 2, 2, 4), ("yk", "y2", "zh", "zl", "core", "x")
    )
    left = P(ROW + ("x",), None, None)
    right = P("x", None, None)
    moments = P(ROW + REP, "x")
    return jax.shard_map(
        shards,
        mesh=fine,
        in_specs=(P(REP, ROW, "x"), left, right, left, right, moments, moments),
        out_specs=(P(ROW, "x"), left, left, right, right, moments, moments),
        check_vma=False,
    )
```
